32 devices in a mesh: user: 8 (over z, y), item: 4 (over x, core).
Axes of the slice: x: 2, y: 2, z: 4, core: 2. Of those that a mesh axis runs over, the one named last changes fastest.
Arguments:
- item_features: bfloat16 [2048, 2048], P(('item', 'user')), may hold values from -6 to 6
- layer_one: bfloat16 [2048, 1024], replicated, may hold values from -0.125 to 0.125
- layer_two: bfloat16 [1024, 512], replicated, may hold values from -0.1875 to 0.1875
- log_weight: float32 [2048], P(('item', 'user')), may hold values from 0 to 4.9
- user_vectors: bfloat16 [4096, 512], P('user'), may hold values from -360 to 360
- positive_index: int32 [4096], P('user'), may hold values from 0 to 2047
Outputs:
- row_loss: float32 [4096], P('user')
- col_lse: float32 [2048], P(('item', 'user'))
The draws below stay inside these ranges and needn't reach their ends.
All inputs are finite; a program needn't handle non-finite values.
Results may differ from the reference program's by a relative error of at most 0.007.
Values may be sent and summed in bfloat16 or wider, within the bound.
A program may use at most 64 MiB of HBM per device.

```python
import math
import jax
import jax.numpy as jnp
from jax import lax

D_IN = 2048
D_HID = 1024
D_EMB = 512
ITEM_DEV = 64
ITEMS = 2048
USERS = 4096
N_USER = 8


def draw_user_vectors(key, part):
    key = jax.random.fold_in(key, 11)
    first = jax.random.fold_in(key, 0)
    base = jnp.clip(jax.random.normal(first, (USERS, D_EMB), jnp.float32), -6.0, 6.0)
    return base.astype(jnp.bfloat16)


def draw_positive_index(key, part):
    key = jax.random.fold_in(key, 23)
    first, second, third = jax.random.split(key, 3)
    chosen = jax.random.randint(first, (USERS,), 0, ITEMS, jnp.int32)
    low_spot = jax.random.randint(second, (), 0, USERS // 2, jnp.int32)
    high_spot = jax.random.randint(third, (), USERS // 2, USERS, jnp.int32)
    chosen = chosen.at[low_spot].set(0)
    chosen = chosen.at[high_spot].set(ITEMS - 1)
    return chosen


def ramped_weight(key, height):
    rough = jax.random.uniform(key, (ITEMS,), jnp.float32, 0.0, 1.5)
    place = jnp.arange(ITEMS, dtype=jnp.float32) / float(ITEMS)
    return rough + height * place


def draw_log_weight(key, part):
    key = jax.random.fold_in(key, 37)
    return ramped_weight(key, math.log(10.0))


def block_scale(rng, dims, cuts, smallest, largest):
    level = 1.0
    for dim, shards_of in cuts:
        heights = jax.random.uniform(jax.random.fold_in(jax.random.fold_in(rng, 6), dim), (shards_of,), jnp.float32, smallest / len(cuts), largest / len(cuts))
        level = level * jnp.repeat(jnp.exp(heights), dims[dim] // shards_of).reshape((-1,) + (1,) * (len(dims) - 1 - dim))
    return level


def noise(own_key, dims, scale, most, pieces=(), kind=jnp.bfloat16):
    values = jax.random.normal(own_key, dims, jnp.float32) * scale
    if len(pieces) > 0:
        values = block_scale(own_key, dims, pieces, -0.22, 0.18) * values
    return jnp.clip(values, min=-most, max=most).astype(kind)


def setup_inputs(seed: int = 0) -> dict:
    key_list = jax.random.split(jax.random.key(seed), 7)
    item_features = noise(key_list[0], (ITEMS, D_IN), 1.0, 6.0, ((0, 32),))
    layer_one = noise(key_list[1], (D_IN, D_HID), D_IN ** -0.5, 0.125)
    layer_two = noise(key_list[2], (D_HID, D_EMB), D_HID ** -0.5, 0.1875)
    log_weight = draw_log_weight(jax.random.fold_in(key_list[6], 71), 0)
    user_vectors = draw_user_vectors(jax.random.fold_in(key_list[6], 71), 0)
    positive_index = draw_positive_index(jax.random.fold_in(key_list[6], 71), 0)
    return dict(item_features=item_features, layer_one=layer_one, layer_two=layer_two, log_weight=log_weight, user_vectors=user_vectors, positive_index=positive_index)


def reference(item_features, layer_one, layer_two, log_weight, user_vectors, positive_index):
    hidden = jax.nn.relu(jnp.dot(item_features, layer_one, preferred_element_type=jnp.float32)).astype(jnp.bfloat16)
    embedded = jnp.dot(hidden, layer_two, preferred_element_type=jnp.float32).astype(jnp.bfloat16)
    block = ITEM_DEV * N_USER
    count = ITEMS // block
    inverse_temp = 4.0 / math.sqrt(D_EMB)
    vectors = embedded.reshape(count, block, D_EMB)
    weights = log_weight.reshape(count, block)
    indices = jnp.arange(count, dtype=jnp.int32)

    def step(carry, inputs):
        row_max, row_sum, row_positive = carry
        piece, piece_weight, index = inputs
        scores = jnp.dot(user_vectors, piece.T, preferred_element_type=jnp.float32) * inverse_temp
        top_col = lax.optimization_barrier(jnp.max(scores, axis=0))
        lse_col = top_col + jnp.log(lax.optimization_barrier(jnp.sum(jnp.exp(scores - top_col[None, :]), axis=0)))
        logits = scores + piece_weight[None, :]
        new_max = jnp.maximum(row_max, lax.optimization_barrier(jnp.max(logits, axis=1)))
        row_sum = row_sum * jnp.exp(row_max - new_max) + lax.optimization_barrier(jnp.sum(jnp.exp(logits - new_max[:, None]), axis=1))
        columns = index * block + jnp.arange(block, dtype=jnp.int32)
        hits = positive_index[:, None] == columns[None, :]
        row_positive = row_positive + lax.optimization_barrier(jnp.sum(jnp.where(hits, logits, jnp.zeros_like(logits)), axis=1))
        return ((new_max, row_sum, row_positive), lse_col)
    start = (jnp.full((USERS,), -1e+30, jnp.float32), jnp.zeros((USERS,), jnp.float32), jnp.zeros((USERS,), jnp.float32))
    carry, columns_lse = lax.scan(step, start, (vectors, weights, indices))
    row_max, row_sum, row_positive = carry
    row_loss = row_max + jnp.log(row_sum) - row_positive
    return (row_loss, columns_lse.reshape(ITEMS))
```

```python
import functools
import math

import jax
import jax.numpy as jnp
from jax import lax
from jax.experimental import pallas as pl
from jax.experimental.pallas import tpu as pltpu
from jax.sharding import PartitionSpec as P

MESH = pl.DeviceIdType.MESH
CHUNKS = 4


def kernel(n_user, n_item, n_y, x_hbm, w1_hbm, w2_hbm, lw_ref, uv_hbm, pos_ref, row_ref, col_ref,
           xv, w1v, w2v, uvv, hv, emb, lwg, col_send, col_recv, row_send, row_recv,
           in_sem, w1_sem, lw_ssem, lw_rsem, z_ssem, y_ssem, emb_rsem, col_ssem, col_rsem, row_ssem, row_rsem):
    n_z = n_user // n_y
    u = lax.axis_index("user")
    i = lax.axis_index("item")
    z, y = u // n_y, u % n_y
    per = xv.shape[0]
    users = uvv.shape[0]
    inverse_temp = 4.0 / math.sqrt(uvv.shape[1])
    wide = hv.shape[1] // CHUNKS

    cx = pltpu.make_async_copy(x_hbm, xv, in_sem.at[0])
    cx.start()
    c1 = []
    for c in range(CHUNKS):
        cols = pl.ds(c * wide, wide)
        c1.append(pltpu.make_async_copy(w1_hbm.at[:, cols], w1v.at[:, cols], w1_sem.at[c]))
        c1[-1].start()
    c2 = pltpu.make_async_copy(w2_hbm, w2v, in_sem.at[1])
    c2.start()
    cu = pltpu.make_async_copy(uv_hbm, uvv, in_sem.at[2])
    cu.start()

    def user_at(d):
        return lax.rem(u + d, n_user)

    def item_at(d):
        return lax.rem(i + d, n_item)

    barrier = pltpu.get_barrier_semaphore()
    for d in range(1, n_user):
        pl.semaphore_signal(barrier, inc=1, device_id={"user": user_at(d)}, device_id_type=MESH)
    for d in range(1, n_item):
        pl.semaphore_signal(barrier, inc=1, device_id={"item": item_at(d)}, device_id_type=MESH)

    def to_user(src, dst, ssem, rsem, t):
        return pltpu.make_async_remote_copy(
            src_ref=src, dst_ref=dst, send_sem=ssem, recv_sem=rsem,
            device_id={"user": t}, device_id_type=MESH)

    def to_item(src, dst, ssem, rsem, t):
        return pltpu.make_async_remote_copy(
            src_ref=src, dst_ref=dst, send_sem=ssem, recv_sem=rsem,
            device_id={"item": t}, device_id_type=MESH)

    lwg[u] = jnp.zeros((8, 128), jnp.float32)
    lwg[u, 0:1, 0:per] = lw_ref[...]

    cx.wait()
    xs = xv[...]
    for c in range(CHUNKS):
        c1[c].wait()
        cols = slice(c * wide, (c + 1) * wide)
        part = jnp.dot(xs, w1v[:, cols], preferred_element_type=jnp.float32)
        hv[:, cols] = jnp.maximum(part, 0.0).astype(jnp.bfloat16)
        if c == CHUNKS - 2:
            pl.semaphore_wait(barrier, n_user + n_item - 2)
            for d in range(1, n_user):
                to_user(lwg.at[u], lwg.at[u], lw_ssem.at[d], lw_rsem.at[u], user_at(d)).start()
    c2.wait()
    emb[u] = jnp.dot(hv[...], w2v[...], preferred_element_type=jnp.float32).astype(jnp.bfloat16)

    def z_piece(d):
        return lax.rem(z + n_z - d, n_z) * n_y + y

    def y_piece(d, e):
        return lax.rem(z + n_z - d, n_z) * n_y + lax.rem(y + n_y - e, n_y)

    def forward(p, d):
        for e in range(1, n_y):
            t = z * n_y + lax.rem(y + e, n_y)
            to_user(emb.at[p], emb.at[p], y_ssem.at[d, e], emb_rsem.at[p], t).start()

    def arrive(p):
        to_user(emb.at[p], emb.at[p], z_ssem.at[0], emb_rsem.at[p], u).wait_recv()

    forward(u, 0)
    for d in range(1, n_z):
        t = lax.rem(z + d, n_z) * n_y + y
        to_user(emb.at[u], emb.at[u], z_ssem.at[d], emb_rsem.at[u], t).start()

    cu.wait()
    for d in range(1, n_user):
        p = user_at(d)
        to_user(lwg.at[p], lwg.at[p], lw_ssem.at[0], lw_rsem.at[p], u).wait_recv()

    eye = (lax.broadcasted_iota(jnp.int32, (per, 128), 0)
           == lax.broadcasted_iota(jnp.int32, (per, 128), 1))
    item_of = lax.broadcasted_iota(jnp.int32, (per, users), 0)
    group_start = i * n_user * per

    def piece(p, own, carry):
        row_max, row_sum, row_pos = carry
        scores = lax.dot_general(emb[p], uvv[...], (((1,), (1,)), ((), ())),
                                 preferred_element_type=jnp.float32) * inverse_temp
        top = jnp.max(scores, axis=1, keepdims=True)
        lse = top + jnp.log(jnp.sum(jnp.exp(scores - top), axis=1, keepdims=True))
        flat = jnp.sum(jnp.where(eye, lse, 0.0), axis=0, keepdims=True)
        tile = jnp.broadcast_to(flat, (8, 128))
        if own:
            col_recv[u] = tile
        else:
            col_send[p] = tile
            to_user(col_send.at[p], col_recv.at[u], col_ssem.at[p], col_rsem.at[u], p).start()
        weight = jnp.sum(jnp.where(eye, lwg[p, 0:1, :], 0.0), axis=1, keepdims=True)
        logits = scores + weight
        new_max = jnp.maximum(row_max, jnp.max(logits, axis=0, keepdims=True))
        row_sum = row_sum * jnp.exp(row_max - new_max) + jnp.sum(
            jnp.exp(logits - new_max), axis=0, keepdims=True)
        hits = pos_ref[...] == group_start + p * per + item_of
        row_pos = row_pos + jnp.sum(jnp.where(hits, logits, 0.0), axis=0, keepdims=True)
        return new_max, row_sum, row_pos

    carry = (jnp.full((1, users), -1e30, jnp.float32), jnp.zeros((1, users), jnp.float32),
             jnp.zeros((1, users), jnp.float32))
    carry = piece(u, True, carry)

    def y_step(d, carry):
        for e in range(1, n_y):
            p = y_piece(d, e)
            arrive(p)
            carry = piece(p, False, carry)
        return carry

    def step(d, carry):
        p = z_piece(d)
        arrive(p)
        forward(p, d)
        carry = piece(p, False, carry)
        return y_step(d - 1, carry)

    if n_user <= 8:
        for d in range(1, n_z):
            carry = step(d, carry)
    else:
        carry = lax.fori_loop(1, n_z, step, carry)
    carry = y_step(n_z - 1, carry)

    row_max, row_sum, row_pos = carry
    row_lse = row_max + jnp.log(row_sum)
    first = lax.broadcasted_iota(jnp.int32, (8, users), 0) == 0
    stats = jnp.where(first, row_lse, row_pos)
    row_send[...] = stats
    for d in range(1, n_item):
        to_item(row_send, row_recv.at[i], row_ssem.at[d], row_rsem.at[i], item_at(d)).start()
    row_recv[i] = stats

    for d in range(1, n_item):
        q = item_at(d)
        to_item(row_send, row_recv.at[q], row_ssem.at[0], row_rsem.at[q], i).wait_recv()
    lse_all = row_recv[:, 0, :]
    top = jnp.max(lse_all, axis=0, keepdims=True)
    total = top + jnp.log(jnp.sum(jnp.exp(lse_all - top), axis=0, keepdims=True))
    row_ref[...] = total - jnp.sum(row_recv[:, 1, :], axis=0, keepdims=True)

    for d in range(1, n_user):
        p = user_at(d)
        to_user(col_send.at[p], col_recv.at[p], col_ssem.at[0], col_rsem.at[p], u).wait_recv()
    lse_all = col_recv[:, 0, :]
    top = jnp.max(lse_all, axis=0, keepdims=True)
    total = top + jnp.log(jnp.sum(jnp.exp(lse_all - top), axis=0, keepdims=True))
    col_ref[...] = total[:, 0:per]

    for d in range(1, n_user):
        p = user_at(d)
        to_user(lwg.at[u], lwg.at[u], lw_ssem.at[d], lw_rsem.at[u], p).wait_send()
        to_user(col_send.at[p], col_recv.at[u], col_ssem.at[p], col_rsem.at[u], p).wait_send()
    for d in range(1, n_item):
        to_item(row_send, row_recv.at[i], row_ssem.at[d], row_rsem.at[i], item_at(d)).wait_send()
    for d in range(n_z):
        if d > 0:
            to_user(emb.at[u], emb.at[u], z_ssem.at[d], emb_rsem.at[u], u).wait_send()
        for e in range(1, n_y):
            to_user(emb.at[u], emb.at[u], y_ssem.at[d, e], emb_rsem.at[u], u).wait_send()


def on_device(n_user, n_item, n_y, item_features, layer_one, layer_two, log_weight, user_vectors,
              positive_index):
    per, d_in = item_features.shape
    d_hid, d_emb = layer_two.shape
    users = user_vectors.shape[0]
    anywhere = pl.BlockSpec(memory_space=pl.ANY)
    vmem = pl.BlockSpec(memory_space=pltpu.VMEM)
    dma = pltpu.SemaphoreType.DMA
    row, col = pl.pallas_call(
        functools.partial(kernel, n_user, n_item, n_y),
        out_shape=(jax.ShapeDtypeStruct((1, users), jnp.float32),
                   jax.ShapeDtypeStruct((1, per), jnp.float32)),
        in_specs=[anywhere, anywhere, anywhere, vmem, anywhere, vmem],
        out_specs=(vmem, vmem),
        scratch_shapes=[
            pltpu.VMEM((per, d_in), jnp.bfloat16),
            pltpu.VMEM((d_in, d_hid), jnp.bfloat16),
            pltpu.VMEM((d_hid, d_emb), jnp.bfloat16),
            pltpu.VMEM((users, d_emb), jnp.bfloat16),
            pltpu.VMEM((per, d_hid), jnp.bfloat16),
            pltpu.VMEM((n_user, per, d_emb), jnp.bfloat16),
            pltpu.VMEM((n_user, 8, 128), jnp.float32),
            pltpu.VMEM((n_user, 8, 128), jnp.float32),
            pltpu.VMEM((n_user, 8, 128), jnp.float32),
            pltpu.VMEM((8, users), jnp.float32),
            pltpu.VMEM((n_item, 8, users), jnp.float32),
            dma((3,)),
            dma((CHUNKS,)),
            dma((n_user,)),
            dma((n_user,)),
            dma((n_user // n_y,)),
            dma((n_user // n_y, n_y)),
            dma((n_user,)),
            dma((n_user,)),
            dma((n_user,)),
            dma((n_item,)),
            dma((n_item,)),
        ],
        compiler_params=pltpu.CompilerParams(
            collective_id=0, has_side_effects=True, vmem_limit_bytes=40 * 1024 * 1024),
    )(item_features, layer_one, layer_two, log_weight.reshape(1, per), user_vectors,
      positive_index.reshape(1, users))
    return row.reshape(users), col.reshape(per)


def solution(mesh):
    n_user, n_item = mesh.shape["user"], mesh.shape["item"]
    n_y = 1
    while n_user % (2 * n_y) == 0 and 8 * n_y * n_y <= n_user:
        n_y *= 2
    placed = (P(("item", "user"), None), P(), P(), P(("item", "user")), P("user", None), P("user"))
    return jax.shard_map(
        functools.partial(on_device, n_user, n_item, n_y),
        mesh=mesh,
        in_specs=placed,
        out_specs=(P("user"), P(("item", "user"))),
        check_vma=False,
    )
```

```python
import functools
import math

import jax
import jax.numpy as jnp
from jax import lax
from jax.experimental import pallas as pl
from jax.experimental.pallas import tpu as pltpu
from jax.sharding import PartitionSpec as P

MESH = pl.DeviceIdType.MESH
CHUNKS = 4


def kernel(n_user, n_item, n_y, x_hbm, w1_hbm, w2_hbm, lw_hbm, uv_hbm, pos_hbm, row_ref, col_ref,
           xv, w1v, w2v, uvv, uvt, lw_ref, pos_ref, hv, emb, lwg, col_send, col_recv, row_send, row_recv,
           in_sem, w1_sem, lw_ssem, lw_rsem, z_ssem, y_ssem, emb_rsem, col_ssem, col_rsem, row_ssem, row_rsem):
    n_z = n_user // n_y
    u = lax.axis_index("user")
    i = lax.axis_index("item")
    z, y = u // n_y, u % n_y
    per = xv.shape[0]
    users = uvv.shape[0]
    inverse_temp = 4.0 / math.sqrt(uvv.shape[1])
    wide = hv.shape[1] // CHUNKS

    cx = pltpu.make_async_copy(x_hbm, xv, in_sem.at[0])
    cx.start()
    c1 = []
    for c in range(CHUNKS):
        cols = pl.ds(c * wide, wide)
        c1.append(pltpu.make_async_copy(w1_hbm.at[:, cols], w1v.at[:, cols], w1_sem.at[c]))
        c1[-1].start()
    c2 = pltpu.make_async_copy(w2_hbm, w2v, in_sem.at[1])
    c2.start()
    cu = pltpu.make_async_copy(uv_hbm, uvv, in_sem.at[2])
    cu.start()
    cp = pltpu.make_async_copy(pos_hbm, pos_ref, in_sem.at[3])
    cp.start()
    cw = pltpu.make_async_copy(lw_hbm, lw_ref, in_sem.at[4])
    cw.start()

    def user_at(d):
        return lax.rem(u + d, n_user)

    def item_at(d):
        return lax.rem(i + d, n_item)

    barrier = pltpu.get_barrier_semaphore()
    for d in range(1, n_user):
        pl.semaphore_signal(barrier, inc=1, device_id={"user": user_at(d)}, device_id_type=MESH)
    for d in range(1, n_item):
        pl.semaphore_signal(barrier, inc=1, device_id={"item": item_at(d)}, device_id_type=MESH)

    def to_user(src, dst, ssem, rsem, t):
        return pltpu.make_async_remote_copy(
            src_ref=src, dst_ref=dst, send_sem=ssem, recv_sem=rsem,
            device_id={"user": t}, device_id_type=MESH)

    def to_item(src, dst, ssem, rsem, t):
        return pltpu.make_async_remote_copy(
            src_ref=src, dst_ref=dst, send_sem=ssem, recv_sem=rsem,
            device_id={"item": t}, device_id_type=MESH)

    lwg[u] = jnp.zeros((8, 128), jnp.float32)
    cw.wait()
    lwg[u, 0:1, 0:per] = lw_ref[...]

    cx.wait()
    xs = xv[...]
    for c in range(CHUNKS):
        c1[c].wait()
        cols = slice(c * wide, (c + 1) * wide)
        part = jnp.dot(xs, w1v[:, cols], preferred_element_type=jnp.float32)
        hv[:, cols] = jnp.maximum(part, 0.0).astype(jnp.bfloat16)
        if c == CHUNKS - 2:
            pl.semaphore_wait(barrier, n_user + n_item - 2)
            for d in range(1, n_user):
                to_user(lwg.at[u], lwg.at[u], lw_ssem.at[d], lw_rsem.at[u], user_at(d)).start()
    c2.wait()
    emb[u] = jnp.dot(hv[...], w2v[...], preferred_element_type=jnp.float32).astype(jnp.bfloat16)

    def z_piece(d):
        return lax.rem(z + n_z - d, n_z) * n_y + y

    def y_piece(d, e):
        return lax.rem(z + n_z - d, n_z) * n_y + lax.rem(y + n_y - e, n_y)

    def forward(p, d):
        for e in range(1, n_y):
            t = z * n_y + lax.rem(y + e, n_y)
            to_user(emb.at[p], emb.at[p], y_ssem.at[d, e], emb_rsem.at[p], t).start()

    def arrive(p):
        to_user(emb.at[p], emb.at[p], z_ssem.at[0], emb_rsem.at[p], u).wait_recv()

    forward(u, 0)
    for d in range(1, n_z):
        t = lax.rem(z + d, n_z) * n_y + y
        to_user(emb.at[u], emb.at[u], z_ssem.at[d], emb_rsem.at[u], t).start()

    cu.wait()
    cp.wait()
    for r in range(0, users, 128):
        uvt[:, r:r + 128] = uvv[r:r + 128, :].T
    for d in range(1, n_user):
        p = user_at(d)
        to_user(lwg.at[p], lwg.at[p], lw_ssem.at[0], lw_rsem.at[p], u).wait_recv()

    eye = (lax.broadcasted_iota(jnp.int32, (per, 128), 0)
           == lax.broadcasted_iota(jnp.int32, (per, 128), 1))
    item_of = lax.broadcasted_iota(jnp.int32, (per, users), 0)
    group_start = i * n_user * per

    def piece(p, own, carry):
        row_max, row_sum, row_pos = carry
        scores = jnp.dot(emb[p], uvt[...], preferred_element_type=jnp.float32) * inverse_temp
        top = jnp.max(scores, axis=1, keepdims=True)
        lse = top + jnp.log(jnp.sum(jnp.exp(scores - top), axis=1, keepdims=True))
        flat = jnp.sum(jnp.where(eye, lse, 0.0), axis=0, keepdims=True)
        tile = jnp.broadcast_to(flat, (8, 128))
        if own:
            col_recv[u] = tile
        else:
            col_send[p] = tile
            to_user(col_send.at[p], col_recv.at[u], col_ssem.at[p], col_rsem.at[u], p).start()
        weight = jnp.sum(jnp.where(eye, lwg[p, 0:1, :], 0.0), axis=1, keepdims=True)
        logits = scores + weight
        new_max = jnp.maximum(row_max, jnp.max(logits, axis=0, keepdims=True))
        row_sum = row_sum * jnp.exp(row_max - new_max) + jnp.sum(
            jnp.exp(logits - new_max), axis=0, keepdims=True)
        hits = pos_ref[...] == group_start + p * per + item_of
        row_pos = row_pos + jnp.sum(jnp.where(hits, logits, 0.0), axis=0, keepdims=True)
        return new_max, row_sum, row_pos

    carry = (jnp.full((1, users), -1e30, jnp.float32), jnp.zeros((1, users), jnp.float32),
             jnp.zeros((1, users), jnp.float32))
    carry = piece(u, True, carry)

    def y_step(d, carry):
        for e in range(1, n_y):
            p = y_piece(d, e)
            arrive(p)
            carry = piece(p, False, carry)
        return carry

    def step(d, carry):
        p = z_piece(d)
        arrive(p)
        forward(p, d)
        carry = piece(p, False, carry)
        return y_step(d - 1, carry)

    if n_user <= 8:
        for d in range(1, n_z):
            carry = step(d, carry)
    else:
        carry = lax.fori_loop(1, n_z, step, carry)
    carry = y_step(n_z - 1, carry)

    row_max, row_sum, row_pos = carry
    row_lse = row_max + jnp.log(row_sum)
    rows = users // 128
    stats = jnp.concatenate([part[:, 128 * k:128 * (k + 1)] for part in (row_lse, row_pos)
                             for k in range(rows)], axis=0)
    row_send[...] = stats
    for d in range(1, n_item):
        to_item(row_send, row_recv.at[i], row_ssem.at[d], row_rsem.at[i], item_at(d)).start()
    row_recv[i] = stats

    for d in range(1, n_item):
        q = item_at(d)
        to_item(row_send, row_recv.at[q], row_ssem.at[0], row_rsem.at[q], i).wait_recv()
    lse_all = row_recv[:, 0:rows, :]
    top = jnp.max(lse_all, axis=0)
    total = top + jnp.log(jnp.sum(jnp.exp(lse_all - top), axis=0))
    row_ref[...] = total - jnp.sum(row_recv[:, rows:2 * rows, :], axis=0)

    for d in range(1, n_user):
        p = user_at(d)
        to_user(col_send.at[p], col_recv.at[p], col_ssem.at[0], col_rsem.at[p], u).wait_recv()
    lse_all = col_recv[:, 0, :]
    top = jnp.max(lse_all, axis=0, keepdims=True)
    total = top + jnp.log(jnp.sum(jnp.exp(lse_all - top), axis=0, keepdims=True))
    col_ref[...] = total[:, 0:per]

    for d in range(1, n_user):
        p = user_at(d)
        to_user(lwg.at[u], lwg.at[u], lw_ssem.at[d], lw_rsem.at[u], p).wait_send()
        to_user(col_send.at[p], col_recv.at[u], col_ssem.at[p], col_rsem.at[u], p).wait_send()
    for d in range(1, n_item):
        to_item(row_send, row_recv.at[i], row_ssem.at[d], row_rsem.at[i], item_at(d)).wait_send()
    for d in range(n_z):
        if d > 0:
            to_user(emb.at[u], emb.at[u], z_ssem.at[d], emb_rsem.at[u], u).wait_send()
        for e in range(1, n_y):
            to_user(emb.at[u], emb.at[u], y_ssem.at[d, e], emb_rsem.at[u], u).wait_send()


def on_device(n_user, n_item, n_y, item_features, layer_one, layer_two, log_weight, user_vectors,
              positive_index):
    per, d_in = item_features.shape
    d_hid, d_emb = layer_two.shape
    users = user_vectors.shape[0]
    anywhere = pl.BlockSpec(memory_space=pltpu.HBM)
    vmem = pl.BlockSpec(memory_space=pltpu.VMEM)
    dma = pltpu.SemaphoreType.DMA
    row, col = pl.pallas_call(
        functools.partial(kernel, n_user, n_item, n_y),
        out_shape=(jax.ShapeDtypeStruct((users // 128, 128), jnp.float32),
                   jax.ShapeDtypeStruct((1, per), jnp.float32)),
        in_specs=[anywhere] * 6,
        out_specs=(vmem, vmem),
        scratch_shapes=[
            pltpu.VMEM((per, d_in), jnp.bfloat16),
            pltpu.VMEM((d_in, d_hid), jnp.bfloat16),
            pltpu.VMEM((d_hid, d_emb), jnp.bfloat16),
            pltpu.VMEM((users, d_emb), jnp.bfloat16),
            pltpu.VMEM((d_emb, users), jnp.bfloat16),
            pltpu.VMEM((1, per), jnp.float32),
            pltpu.VMEM((1, users), jnp.int32),
            pltpu.VMEM((per, d_hid), jnp.bfloat16),
            pltpu.VMEM((n_user, per, d_emb), jnp.bfloat16),
            pltpu.VMEM((n_user, 8, 128), jnp.float32),
            pltpu.VMEM((n_user, 8, 128), jnp.float32),
            pltpu.VMEM((n_user, 8, 128), jnp.float32),
            pltpu.VMEM((users // 64, 128), jnp.float32),
            pltpu.VMEM((n_item, users // 64, 128), jnp.float32),
            dma((5,)),
            dma((CHUNKS,)),
            dma((n_user,)),
            dma((n_user,)),
            dma((n_user // n_y,)),
            dma((n_user // n_y, n_y)),
            dma((n_user,)),
            dma((n_user,)),
            dma((n_user,)),
            dma((n_item,)),
            dma((n_item,)),
        ],
        compiler_params=pltpu.CompilerParams(
            collective_id=0, has_side_effects=True, vmem_limit_bytes=62 * 1024 * 1024),
    )(item_features, layer_one, layer_two, log_weight.reshape(1, per), user_vectors,
      positive_index.reshape(1, users))
    return row.reshape(users), col.reshape(per)


def solution(mesh):
    n_user, n_item = mesh.shape["user"], mesh.shape["item"]
    n_y = 1
    while n_user % (2 * n_y) == 0 and 8 * n_y * n_y <= n_user:
        n_y *= 2
    placed = (P(("item", "user"), None), P(), P(), P(("item", "user")), P("user", None), P("user"))
    return jax.shard_map(
        functools.partial(on_device, n_user, n_item, n_y),
        mesh=mesh,
        in_specs=placed,
        out_specs=(P("user"), P(("item", "user"))),
        check_vma=False,
    )
```

```python
import functools
import math

import jax
import jax.numpy as jnp
from jax import lax
from jax.experimental import pallas as pl
from jax.experimental.pallas import tpu as pltpu
from jax.sharding import PartitionSpec as P

MESH = pl.DeviceIdType.MESH
CHUNKS = 4
PARTS = 2


def kernel(n_user, n_item, n_y, x_hbm, w1_hbm, w2_hbm, lw_hbm, uv_hbm, pos_hbm, row_ref, col_ref,
           xv, w1v, w2v, uvb, uvt, posb, lwv, emb, lwg, col_part, col_send, col_recv, row_send, row_recv,
           in_sem, w1_sem, lw_ssem, lw_rsem, emb_ssem, emb_rsem, col_ssem, col_rsem,
           uv_ssem, uv_rsem, pos_ssem, pos_rsem, row_ssem, row_rsem):
    n_z = n_user // n_y
    u = lax.axis_index("user")
    i = lax.axis_index("item")
    z, y = u // n_y, u % n_y
    core = lax.rem(i, 2)
    mate = i + 1 - 2 * core
    per = xv.shape[0]
    users = uvb.shape[1]
    half = users // 2
    sub = half // PARTS
    rows = users // 128
    inverse_temp = 4.0 / math.sqrt(uvb.shape[2])
    deep = w1v.shape[0] // CHUNKS

    cx = pltpu.make_async_copy(x_hbm, xv, in_sem.at[0])
    cx.start()
    c1 = []
    for c in range(CHUNKS):
        part = pl.ds(c * deep, deep)
        c1.append(pltpu.make_async_copy(w1_hbm.at[part], w1v.at[part], w1_sem.at[c]))
        c1[-1].start()
    c2 = pltpu.make_async_copy(w2_hbm, w2v, in_sem.at[1])
    c2.start()
    cu = pltpu.make_async_copy(uv_hbm, uvb.at[0], in_sem.at[2])
    cu.start()
    cp = pltpu.make_async_copy(pos_hbm, posb.at[0], in_sem.at[3])
    cp.start()
    cw = pltpu.make_async_copy(lw_hbm, lwv, in_sem.at[4])
    cw.start()

    def z_to(d):
        return {"user": lax.rem(z + d, n_z) * n_y + y}

    def y_to(e):
        return {"user": z * n_y + lax.rem(y + e, n_y)}

    def plane_to(k, e):
        return {"user": z * n_y + lax.rem(y + e, n_y), "item": lax.rem(i + k, n_item)}

    plane = [(k, e) for e in range(n_y - 1, -1, -1) for k in range(n_item) if (k, e) != (0, 0)]

    barrier = pltpu.get_barrier_semaphore()
    for d in range(1, n_z):
        pl.semaphore_signal(barrier, inc=1, device_id=z_to(d), device_id_type=MESH)
    for k, e in plane:
        pl.semaphore_signal(barrier, inc=1, device_id=plane_to(k, e), device_id_type=MESH)

    def remote(src, dst, ssem, rsem, to):
        return pltpu.make_async_remote_copy(src_ref=src, dst_ref=dst, send_sem=ssem, recv_sem=rsem,
                                            device_id=to, device_id_type=MESH)

    def lw_copy(d):
        return remote(lwg.at[0], lwg.at[d], lw_ssem.at[d], lw_rsem.at[d], z_to(d))

    def emb_copy(d):
        return remote(emb.at[0], emb.at[d], emb_ssem.at[d], emb_rsem.at[d], z_to(d))

    def col_copy(d):
        return remote(col_send.at[d], col_recv.at[d], col_ssem.at[d], col_rsem.at[d], z_to(n_z - d))

    def uv_copy(e, s):
        part = pl.ds(pl.multiple_of(core * half + s * sub, sub), sub)
        return remote(uv_hbm.at[part], uvb.at[e, part], uv_ssem.at[e, 0, s], uv_rsem.at[e, 0, s], y_to(e))

    def uv_share(e, s):
        part = pl.ds(pl.multiple_of(core * half + s * sub, sub), sub)
        return remote(uvb.at[e, part], uvb.at[e, part], uv_ssem.at[e, 1, s], uv_rsem.at[e, 1, s],
                      {"item": mate})

    def pos_copy(e):
        return remote(pos_hbm, posb.at[e], pos_ssem.at[e], pos_rsem.at[e], y_to(e))

    def row_copy(k, e):
        return remote(row_send.at[e], row_recv.at[k, e], row_ssem.at[k, e], row_rsem.at[k, e],
                      plane_to(k, e))

    lwg[0] = jnp.zeros((8, 128), jnp.float32)
    cw.wait()
    lwg[0, 0:1, 0:per] = lwv[...]

    cx.wait()
    hidden = None
    for c in range(CHUNKS):
        c1[c].wait()
        part = jnp.dot(xv[:, c * deep:(c + 1) * deep], w1v[c * deep:(c + 1) * deep, :],
                       preferred_element_type=jnp.float32)
        hidden = part if c == 0 else hidden + part
        if c == 0:
            pl.semaphore_wait(barrier, n_z - 1 + len(plane))
            for s in range(PARTS):
                for e in range(1, n_y):
                    uv_copy(e, s).start()
            for e in range(1, n_y):
                pos_copy(e).start()
            for d in range(1, n_z):
                lw_copy(d).start()
    hidden = jnp.maximum(hidden, 0.0).astype(jnp.bfloat16)
    c2.wait()
    emb[0] = jnp.dot(hidden, w2v[...], preferred_element_type=jnp.float32).astype(jnp.bfloat16)
    for d in range(1, n_z):
        emb_copy(d).start()

    eye = (lax.broadcasted_iota(jnp.int32, (per, 128), 0)
           == lax.broadcasted_iota(jnp.int32, (per, 128), 1))
    item_of = lax.broadcasted_iota(jnp.int32, (per, users), 0)

    def turn(e):
        for r in range(0, users, 128):
            uvt[e, :, r:r + 128] = uvb[e, r:r + 128, :].T

    def block(d, e, carry):
        row_max, row_sum, row_pos = carry
        scores = jnp.dot(emb[d], uvt[e], preferred_element_type=jnp.float32) * inverse_temp
        top = jnp.max(scores, axis=1, keepdims=True)
        lse = top + jnp.log(jnp.sum(jnp.exp(scores - top), axis=1, keepdims=True))
        col_part[d, e:e + 1, :] = jnp.sum(jnp.where(eye, lse, 0.0), axis=0, keepdims=True)
        weight = jnp.sum(jnp.where(eye, lwg[d, 0:1, :], 0.0), axis=1, keepdims=True)
        logits = scores + weight
        new_max = jnp.maximum(row_max, jnp.max(logits, axis=0, keepdims=True))
        row_sum = row_sum * jnp.exp(row_max - new_max) + jnp.sum(
            jnp.exp(logits - new_max), axis=0, keepdims=True)
        start = (i * n_user + lax.rem(z + n_z - d, n_z) * n_y + y) * per
        hits = posb[e] == start + item_of
        row_pos = row_pos + jnp.sum(jnp.where(hits, logits, 0.0), axis=0, keepdims=True)
        return new_max, row_sum, row_pos

    def joined(parts):
        top = jnp.max(parts, axis=0, keepdims=True)
        return top + jnp.log(jnp.sum(jnp.exp(parts - top), axis=0, keepdims=True))

    def col_stats(d):
        return jnp.broadcast_to(joined(col_part[d, 0:n_y, :]), (8, 128))

    def send_col(d):
        col_send[d] = col_stats(d)
        col_copy(d).start()

    def loop(low, high, step, carry):
        if n_z <= 4:
            for d in range(low, high):
                carry = step(d, carry)
            return carry
        return lax.fori_loop(low, high, step, carry)

    empty = (jnp.full((1, users), -1e30, jnp.float32), jnp.zeros((1, users), jnp.float32),
             jnp.zeros((1, users), jnp.float32))

    cu.wait()
    cp.wait()
    turn(0)
    own = block(0, 0, empty)

    def own_step(d, carry):
        lw_copy(d).wait_recv()
        emb_copy(d).wait_recv()
        return block(d, 0, carry)

    last = n_z - 1
    for s in range(PARTS):
        for e in range(1, n_y):
            uv_copy(e, s).wait_recv()
            uv_share(e, s).start()
        if s == 0:
            own = loop(1, min(2, last), own_step, own)
    own = loop(min(2, last), last, own_step, own)

    others = []
    for e in range(1, n_y):
        pos_copy(e).wait_recv()
        for s in range(PARTS):
            uv_share(e, s).wait_recv()
        turn(e)
        others.append(loop(0, last, lambda d, carry, e=e: block(d, e, carry), empty))

    def send_step(d, carry):
        send_col(d)
        return carry

    loop(1, last, send_step, 0)
    if last > 0:
        own = own_step(last, own)
        others = [block(last, e, others[e - 1]) for e in range(1, n_y)]
        send_col(last)
    col_recv[0] = col_stats(0)

    for e, carry in enumerate([own] + others):
        row_max, row_sum, row_pos = carry
        row_lse = row_max + jnp.log(row_sum)
        row_send[(n_y - e) % n_y] = jnp.concatenate(
            [part[:, 128 * k:128 * (k + 1)] for part in (row_lse, row_pos) for k in range(rows)], axis=0)
    for k, e in plane:
        row_copy(k, e).start()
    row_recv[0, 0] = row_send[0]

    for d in range(1, n_z):
        col_copy(d).wait_recv()
    col_ref[...] = joined(col_recv[:, 0, :])[:, 0:per]

    for k, e in plane:
        row_copy(k, e).wait_recv()
    stats = row_recv[...].reshape(n_item * n_y, 2 * rows, 128)
    lse_all = stats[:, 0:rows, :]
    top = jnp.max(lse_all, axis=0)
    total = top + jnp.log(jnp.sum(jnp.exp(lse_all - top), axis=0))
    row_ref[...] = total - jnp.sum(stats[:, rows:2 * rows, :], axis=0)

    for d in range(1, n_z):
        lw_copy(d).wait_send()
        emb_copy(d).wait_send()
        col_copy(d).wait_send()
    for e in range(1, n_y):
        pos_copy(e).wait_send()
        for s in range(PARTS):
            uv_copy(e, s).wait_send()
            uv_share(e, s).wait_send()
    for k, e in plane:
        row_copy(k, e).wait_send()


def hand_out(row_in, col_in, row_out, col_out, sem):
    first = pltpu.make_async_copy(row_in, row_out, sem.at[0])
    second = pltpu.make_async_copy(col_in, col_out, sem.at[1])
    first.start()
    second.start()
    first.wait()
    second.wait()


def on_device(n_user, n_item, n_y, item_features, layer_one, layer_two, log_weight, user_vectors,
              positive_index):
    per, d_in = item_features.shape
    d_hid, d_emb = layer_two.shape
    users = user_vectors.shape[0]
    n_z = n_user // n_y
    rows = users // 128
    anywhere = pl.BlockSpec(memory_space=pltpu.HBM)
    vmem = pl.BlockSpec(memory_space=pltpu.VMEM)
    dma = pltpu.SemaphoreType.DMA
    shapes = (jax.ShapeDtypeStruct((rows, 128), jnp.float32),
              jax.ShapeDtypeStruct((1, per), jnp.float32))
    row, col = pl.pallas_call(
        functools.partial(kernel, n_user, n_item, n_y),
        out_shape=shapes,
        in_specs=[anywhere] * 6,
        out_specs=(vmem, vmem),
        scratch_shapes=[
            pltpu.VMEM((per, d_in), jnp.bfloat16),
            pltpu.VMEM((d_in, d_hid), jnp.bfloat16),
            pltpu.VMEM((d_hid, d_emb), jnp.bfloat16),
            pltpu.VMEM((n_y, users, d_emb), jnp.bfloat16),
            pltpu.VMEM((n_y, d_emb, users), jnp.bfloat16),
            pltpu.VMEM((n_y, 1, users), jnp.int32),
            pltpu.VMEM((1, per), jnp.float32),
            pltpu.VMEM((n_z, per, d_emb), jnp.bfloat16),
            pltpu.VMEM((n_z, 8, 128), jnp.float32),
            pltpu.VMEM((n_z, 8, 128), jnp.float32),
            pltpu.VMEM((n_z, 8, 128), jnp.float32),
            pltpu.VMEM((n_z, 8, 128), jnp.float32),
            pltpu.VMEM((n_y, 2 * rows, 128), jnp.float32),
            pltpu.VMEM((n_item, n_y, 2 * rows, 128), jnp.float32),
            dma((5,)),
            dma((CHUNKS,)),
            dma((n_z,)),
            dma((n_z,)),
            dma((n_z,)),
            dma((n_z,)),
            dma((n_z,)),
            dma((n_z,)),
            dma((n_y, 2, PARTS)),
            dma((n_y, 2, PARTS)),
            dma((n_y,)),
            dma((n_y,)),
            dma((n_item, n_y)),
            dma((n_item, n_y)),
        ],
        compiler_params=pltpu.CompilerParams(
            collective_id=0, has_side_effects=True, vmem_limit_bytes=62 * 1024 * 1024),
    )(item_features, layer_one, layer_two, log_weight.reshape(1, per), user_vectors,
      positive_index.reshape(1, users))
    row, col = pl.pallas_call(
        hand_out,
        out_shape=shapes,
        in_specs=[anywhere] * 2,
        out_specs=(anywhere, anywhere),
        scratch_shapes=[dma((2,))],
        compiler_params=pltpu.CompilerParams(vmem_limit_bytes=62 * 1024 * 1024),
    )(row, col)
    return row.reshape(users), col.reshape(per)


def solution(mesh):
    n_user, n_item = mesh.shape["user"], mesh.shape["item"]
    n_y = 1
    while n_user % (2 * n_y) == 0 and 8 * n_y * n_y <= n_user:
        n_y *= 2
    placed = (P(("item", "user"), None), P(), P(), P(("item", "user")), P("user", None), P("user"))
    return jax.shard_map(
        functools.partial(on_device, n_user, n_item, n_y),
        mesh=mesh,
        in_specs=placed,
        out_specs=(P("user"), P(("item", "user"))),
        check_vma=False,
    )
```

```python
import functools
import math

import jax
import jax.numpy as jnp
from jax import lax
from jax.experimental import pallas as pl
from jax.experimental.pallas import tpu as pltpu
from jax.sharding import PartitionSpec as P

MESH = pl.DeviceIdType.MESH
CHUNKS = 4
PARTS = 2


def kernel(n_user, n_item, n_y, x_hbm, w1_hbm, w2_hbm, lw_hbm, uv_hbm, pos_hbm, row_ref, col_ref,
           xv, w1v, w2v, uvb, uvt, posb, lwv, emb, lwg, col_part, col_send, col_recv, row_send, row_recv,
           in_sem, w1_sem, lw_ssem, lw_rsem, emb_ssem, emb_rsem, col_ssem, col_rsem,
           uv_ssem, uv_rsem, pos_ssem, pos_rsem, row_ssem, row_rsem):
    n_z = n_user // n_y
    u = lax.axis_index("user")
    i = lax.axis_index("item")
    z, y = u // n_y, u % n_y
    core = lax.rem(i, 2)
    mate = i + 1 - 2 * core
    per = xv.shape[0]
    users, d_emb = uvb.shape
    half = users // 2
    sub = d_emb // PARTS
    rows = users // 128
    inverse_temp = 4.0 / math.sqrt(d_emb)
    deep = w1v.shape[0] // CHUNKS

    cu = pltpu.make_async_copy(uv_hbm, uvb, in_sem.at[2])
    cu.start()
    cx = pltpu.make_async_copy(x_hbm, xv, in_sem.at[0])
    cx.start()
    cw = pltpu.make_async_copy(lw_hbm, lwv, in_sem.at[4])
    cw.start()
    c1 = []
    for c in range(CHUNKS):
        part = pl.ds(c * deep, deep)
        c1.append(pltpu.make_async_copy(w1_hbm.at[part], w1v.at[part], w1_sem.at[c]))
        c1[-1].start()
    c2 = pltpu.make_async_copy(w2_hbm, w2v, in_sem.at[1])
    c2.start()
    cp = pltpu.make_async_copy(pos_hbm, posb.at[0], in_sem.at[3])
    cp.start()

    def z_to(d):
        return {"user": lax.rem(z + d, n_z) * n_y + y}

    def y_to(e):
        return {"user": z * n_y + lax.rem(y + e, n_y)}

    def plane_to(k, e):
        return {"user": z * n_y + lax.rem(y + e, n_y), "item": lax.rem(i + k, n_item)}

    plane = [(k, e) for e in range(n_y - 1, -1, -1) for k in range(n_item) if (k, e) != (0, 0)]

    barrier = pltpu.get_barrier_semaphore()
    for d in range(1, n_z):
        pl.semaphore_signal(barrier, inc=1, device_id=z_to(d), device_id_type=MESH)
    for k, e in plane:
        pl.semaphore_signal(barrier, inc=1, device_id=plane_to(k, e), device_id_type=MESH)

    def remote(src, dst, ssem, rsem, to):
        return pltpu.make_async_remote_copy(src_ref=src, dst_ref=dst, send_sem=ssem, recv_sem=rsem,
                                            device_id=to, device_id_type=MESH)

    def lw_copy(d):
        return remote(lwg.at[0], lwg.at[d], lw_ssem.at[d], lw_rsem.at[d], z_to(d))

    def emb_copy(d):
        return remote(emb.at[0], emb.at[d], emb_ssem.at[d], emb_rsem.at[d], z_to(d))

    def col_copy(d):
        return remote(col_send.at[d], col_recv.at[d], col_ssem.at[d], col_rsem.at[d], z_to(n_z - d))

    def uv_copy(e, s):
        part = pl.ds(s * sub, sub)
        return remote(uvt.at[0, core, part], uvt.at[e, core, part],
                      uv_ssem.at[e, 0, s], uv_rsem.at[e, 0, s], y_to(e))

    def uv_share(e, s):
        part = pl.ds(s * sub, sub)
        return remote(uvt.at[e, core, part], uvt.at[e, core, part],
                      uv_ssem.at[e, 1, s], uv_rsem.at[e, 1, s], {"item": mate})

    def pos_copy(e):
        return remote(pos_hbm, posb.at[e], pos_ssem.at[e], pos_rsem.at[e], y_to(e))

    def row_copy(k, e):
        return remote(row_send.at[e], row_recv.at[k, e], row_ssem.at[k, e], row_rsem.at[k, e],
                      plane_to(k, e))

    lwg[0] = jnp.zeros((8, 128), jnp.float32)
    cw.wait()
    lwg[0, 0:1, 0:per] = lwv[...]

    def turn(h):
        uvt[0, h] = uvb[pl.ds(pl.multiple_of(h * half, half), half), :].T

    cu.wait()
    turn(core)
    pl.semaphore_wait(barrier, n_z - 1 + len(plane))
    for s in range(PARTS):
        for e in range(1, n_y):
            uv_copy(e, s).start()
    for d in range(1, n_z):
        lw_copy(d).start()
    for e in range(1, n_y):
        pos_copy(e).start()
    turn(1 - core)

    cx.wait()
    hidden = None
    for c in range(CHUNKS):
        c1[c].wait()
        part = jnp.dot(xv[:, c * deep:(c + 1) * deep], w1v[c * deep:(c + 1) * deep, :],
                       preferred_element_type=jnp.float32)
        hidden = part if c == 0 else hidden + part
    hidden = jnp.maximum(hidden, 0.0).astype(jnp.bfloat16)
    c2.wait()
    emb[0] = jnp.dot(hidden, w2v[...], preferred_element_type=jnp.float32).astype(jnp.bfloat16)
    for d in range(1, n_z):
        emb_copy(d).start()

    eye = (lax.broadcasted_iota(jnp.int32, (per, 128), 0)
           == lax.broadcasted_iota(jnp.int32, (per, 128), 1))
    item_of = lax.broadcasted_iota(jnp.int32, (per, half), 0)

    def block(d, e, slot, h, carry):
        row_max, row_sum, row_pos = carry
        scores = jnp.dot(emb[d], uvt[e, h], preferred_element_type=jnp.float32) * inverse_temp
        top = jnp.max(scores, axis=1, keepdims=True)
        lse = top + jnp.log(jnp.sum(jnp.exp(scores - top), axis=1, keepdims=True))
        row = 2 * e + slot
        col_part[d, row:row + 1, :] = jnp.sum(jnp.where(eye, lse, 0.0), axis=0, keepdims=True)
        weight = jnp.sum(jnp.where(eye, lwg[d, 0:1, :], 0.0), axis=1, keepdims=True)
        logits = scores + weight
        new_max = jnp.maximum(row_max, jnp.max(logits, axis=0, keepdims=True))
        row_sum = row_sum * jnp.exp(row_max - new_max) + jnp.sum(
            jnp.exp(logits - new_max), axis=0, keepdims=True)
        start = (i * n_user + lax.rem(z + n_z - d, n_z) * n_y + y) * per
        hits = posb[e, h] == start + item_of
        row_pos = row_pos + jnp.sum(jnp.where(hits, logits, 0.0), axis=0, keepdims=True)
        return new_max, row_sum, row_pos

    def joined(parts):
        top = jnp.max(parts, axis=0, keepdims=True)
        return top + jnp.log(jnp.sum(jnp.exp(parts - top), axis=0, keepdims=True))

    def col_stats(d):
        return jnp.broadcast_to(joined(col_part[d, 0:2 * n_y, :]), (8, 128))

    def send_col(d):
        col_send[d] = col_stats(d)
        col_copy(d).start()

    def loop(low, high, step, carry):
        if n_z <= 4:
            for d in range(low, high):
                carry = step(d, carry)
            return carry
        return lax.fori_loop(low, high, step, carry)

    empty = (jnp.full((1, half), -1e30, jnp.float32), jnp.zeros((1, half), jnp.float32),
             jnp.zeros((1, half), jnp.float32))

    def own_block(d, carry):
        return tuple(block(d, 0, h, h, carry[h]) for h in range(2))

    def own_step(d, carry):
        lw_copy(d).wait_recv()
        emb_copy(d).wait_recv()
        return own_block(d, carry)

    halves = (core, 1 - core)
    last = n_z - 1
    cp.wait()
    own = own_block(0, (empty, empty))
    for s in range(PARTS):
        for e in range(1, n_y):
            uv_copy(e, s).wait_recv()
            uv_share(e, s).start()
        if s == 0:
            own = loop(1, min(2, last), own_step, own)
    others = []
    for e in range(1, n_y):
        pos_copy(e).wait_recv()
        others.append([loop(0, min(2, last), lambda d, carry, e=e: block(d, e, 0, halves[0], carry), empty)])
    own = loop(min(2, last), last, own_step, own)
    for e in range(1, n_y):
        for s in range(PARTS):
            uv_share(e, s).wait_recv()
    for e in range(1, n_y):
        first = others[e - 1][0]
        others[e - 1] = [
            loop(min(2, last), last, lambda d, carry, e=e: block(d, e, 0, halves[0], carry), first),
            loop(0, last, lambda d, carry, e=e: block(d, e, 1, halves[1], carry), empty)]

    def send_step(d, carry):
        send_col(d)
        return carry

    loop(1, last, send_step, 0)
    if last > 0:
        own = own_step(last, own)
        others = [[block(last, e, k, halves[k], others[e - 1][k]) for k in range(2)]
                  for e in range(1, n_y)]
        send_col(last)
    col_recv[0] = col_stats(0)

    for e, carry in enumerate([own] + others):
        stats = [(row_max + jnp.log(row_sum), row_pos) for row_max, row_sum, row_pos in carry]
        if e > 0:
            low = [jnp.where(core == 0, a, b) for a, b in zip(*stats)]
            high = [jnp.where(core == 0, b, a) for a, b in zip(*stats)]
            stats = [low, high]
        row_send[(n_y - e) % n_y] = jnp.concatenate(
            [stats[h][m][:, 128 * k:128 * (k + 1)] for m in range(2) for h in range(2)
             for k in range(rows // 2)], axis=0)
    for k, e in plane:
        row_copy(k, e).start()
    row_recv[0, 0] = row_send[0]

    for d in range(1, n_z):
        col_copy(d).wait_recv()
    col_ref[...] = joined(col_recv[:, 0, :])[:, 0:per]

    for k, e in plane:
        row_copy(k, e).wait_recv()
    stats = row_recv[...].reshape(n_item * n_y, 2 * rows, 128)
    lse_all = stats[:, 0:rows, :]
    top = jnp.max(lse_all, axis=0)
    total = top + jnp.log(jnp.sum(jnp.exp(lse_all - top), axis=0))
    row_ref[...] = total - jnp.sum(stats[:, rows:2 * rows, :], axis=0)

    for d in range(1, n_z):
        lw_copy(d).wait_send()
        emb_copy(d).wait_send()
        col_copy(d).wait_send()
    for e in range(1, n_y):
        pos_copy(e).wait_send()
        for s in range(PARTS):
            uv_copy(e, s).wait_send()
            uv_share(e, s).wait_send()
    for k, e in plane:
        row_copy(k, e).wait_send()


def hand_out(row_in, col_in, row_out, col_out, sem):
    first = pltpu.make_async_copy(row_in, row_out, sem.at[0])
    second = pltpu.make_async_copy(col_in, col_out, sem.at[1])
    first.start()
    second.start()
    first.wait()
    second.wait()


def on_device(n_user, n_item, n_y, item_features, layer_one, layer_two, log_weight, user_vectors,
              positive_index):
    per, d_in = item_features.shape
    d_hid, d_emb = layer_two.shape
    users = user_vectors.shape[0]
    n_z = n_user // n_y
    rows = users // 128
    anywhere = pl.BlockSpec(memory_space=pltpu.HBM)
    vmem = pl.BlockSpec(memory_space=pltpu.VMEM)
    dma = pltpu.SemaphoreType.DMA
    shapes = (jax.ShapeDtypeStruct((rows, 128), jnp.float32),
              jax.ShapeDtypeStruct((1, per), jnp.float32))
    row, col = pl.pallas_call(
        functools.partial(kernel, n_user, n_item, n_y),
        out_shape=shapes,
        in_specs=[anywhere] * 6,
        out_specs=(vmem, vmem),
        scratch_shapes=[
            pltpu.VMEM((per, d_in), jnp.bfloat16),
            pltpu.VMEM((d_in, d_hid), jnp.bfloat16),
            pltpu.VMEM((d_hid, d_emb), jnp.bfloat16),
            pltpu.VMEM((users, d_emb), jnp.bfloat16),
            pltpu.VMEM((n_y, 2, d_emb, users // 2), jnp.bfloat16),
            pltpu.VMEM((n_y, 2, 1, users // 2), jnp.int32),
            pltpu.VMEM((1, per), jnp.float32),
            pltpu.VMEM((n_z, per, d_emb), jnp.bfloat16),
            pltpu.VMEM((n_z, 8, 128), jnp.float32),
            pltpu.VMEM((n_z, 8, 128), jnp.float32),
            pltpu.VMEM((n_z, 8, 128), jnp.float32),
            pltpu.VMEM((n_z, 8, 128), jnp.float32),
            pltpu.VMEM((n_y, 2 * rows, 128), jnp.float32),
            pltpu.VMEM((n_item, n_y, 2 * rows, 128), jnp.float32),
            dma((5,)),
            dma((CHUNKS,)),
            dma((n_z,)),
            dma((n_z,)),
            dma((n_z,)),
            dma((n_z,)),
            dma((n_z,)),
            dma((n_z,)),
            dma((n_y, 2, PARTS)),
            dma((n_y, 2, PARTS)),
            dma((n_y,)),
            dma((n_y,)),
            dma((n_item, n_y)),
            dma((n_item, n_y)),
        ],
        compiler_params=pltpu.CompilerParams(
            collective_id=0, has_side_effects=True, vmem_limit_bytes=62 * 1024 * 1024),
    )(item_features, layer_one, layer_two, log_weight.reshape(1, per), user_vectors,
      positive_index.reshape(2, 1, users // 2))
    row, col = pl.pallas_call(
        hand_out,
        out_shape=shapes,
        in_specs=[anywhere] * 2,
        out_specs=(anywhere, anywhere),
        scratch_shapes=[dma((2,))],
        compiler_params=pltpu.CompilerParams(vmem_limit_bytes=62 * 1024 * 1024),
    )(row, col)
    return row.reshape(users), col.reshape(per)


def solution(mesh):
    n_user, n_item = mesh.shape["user"], mesh.shape["item"]
    n_y = 1
    while n_user % (2 * n_y) == 0 and 8 * n_y * n_y <= n_user:
        n_y *= 2
    placed = (P(("item", "user"), None), P(), P(), P(("item", "user")), P("user", None), P("user"))
    return jax.shard_map(
        functools.partial(on_device, n_user, n_item, n_y),
        mesh=mesh,
        in_specs=placed,
        out_specs=(P("user"), P(("item", "user"))),
        check_vma=False,
    )
```

```python
import functools
import math

import jax
import jax.numpy as jnp
from jax import lax
from jax.experimental import pallas as pl
from jax.experimental.pallas import tpu as pltpu
from jax.sharding import PartitionSpec as P

MESH = pl.DeviceIdType.MESH
CHUNKS = 4
PARTS = 2


def kernel(n_user, n_item, n_y, x_hbm, w1_hbm, w2_hbm, lw_hbm, uv_hbm, pos_hbm, row_ref, col_ref,
           xv, w1v, w2v, uvb, uvt, posb, lwv, emb, lwg, col_part, col_send, col_recv, row_send, row_recv,
           in_sem, w1_sem, lw_ssem, lw_rsem, emb_ssem, emb_rsem, col_ssem, col_rsem,
           uv_ssem, uv_rsem, pos_ssem, pos_rsem, row_ssem, row_rsem):
    n_z = n_user // n_y
    u = lax.axis_index("user")
    i = lax.axis_index("item")
    z, y = u // n_y, u % n_y
    core = lax.rem(i, 2)
    mate = i + 1 - 2 * core
    per = xv.shape[0]
    users, d_emb = uvb.shape
    half = users // 2
    sub = d_emb // PARTS
    rows = users // 128
    inverse_temp = 4.0 / math.sqrt(d_emb)
    deep = w1v.shape[0] // CHUNKS

    cu = pltpu.make_async_copy(uv_hbm, uvb, in_sem.at[2])
    cu.start()
    cx = pltpu.make_async_copy(x_hbm, xv, in_sem.at[0])
    cx.start()
    cw = pltpu.make_async_copy(lw_hbm, lwv, in_sem.at[4])
    cw.start()
    c1 = []
    for c in range(CHUNKS):
        part = pl.ds(c * deep, deep)
        c1.append(pltpu.make_async_copy(w1_hbm.at[part], w1v.at[part], w1_sem.at[c]))
        c1[-1].start()
    c2 = pltpu.make_async_copy(w2_hbm, w2v, in_sem.at[1])
    c2.start()
    cp = pltpu.make_async_copy(pos_hbm, posb.at[0], in_sem.at[3])
    cp.start()

    def z_to(d):
        return {"user": lax.rem(z + d, n_z) * n_y + y}

    def y_to(e):
        return {"user": z * n_y + lax.rem(y + e, n_y)}

    def plane_to(k, e):
        return {"user": z * n_y + lax.rem(y + e, n_y), "item": lax.rem(i + k, n_item)}

    plane = [(k, e) for e in range(n_y - 1, -1, -1) for k in range(n_item) if (k, e) != (0, 0)]

    barrier = pltpu.get_barrier_semaphore()
    for d in range(1, n_z):
        pl.semaphore_signal(barrier, inc=1, device_id=z_to(d), device_id_type=MESH)
    for k, e in plane:
        pl.semaphore_signal(barrier, inc=1, device_id=plane_to(k, e), device_id_type=MESH)

    def remote(src, dst, ssem, rsem, to):
        return pltpu.make_async_remote_copy(src_ref=src, dst_ref=dst, send_sem=ssem, recv_sem=rsem,
                                            device_id=to, device_id_type=MESH)

    def lw_copy(d):
        return remote(lwg.at[0], lwg.at[d], lw_ssem.at[d], lw_rsem.at[d], z_to(d))

    def emb_copy(d):
        return remote(emb.at[0], emb.at[d], emb_ssem.at[d], emb_rsem.at[d], z_to(d))

    def col_copy(d):
        return remote(col_send.at[d], col_recv.at[d], col_ssem.at[d], col_rsem.at[d], z_to(n_z - d))

    def uv_copy(e, s):
        part = pl.ds(s * sub, sub)
        return remote(uvt.at[0, core, part], uvt.at[e, core, part],
                      uv_ssem.at[e, 0, s], uv_rsem.at[e, 0, s], y_to(e))

    def uv_share(e, s):
        part = pl.ds(s * sub, sub)
        return remote(uvt.at[e, core, part], uvt.at[e, core, part],
                      uv_ssem.at[e, 1, s], uv_rsem.at[e, 1, s], {"item": mate})

    def pos_copy(e):
        return remote(pos_hbm, posb.at[e], pos_ssem.at[e], pos_rsem.at[e], y_to(e))

    def row_copy(k, e):
        return remote(row_send.at[e], row_recv.at[k, e], row_ssem.at[k, e], row_rsem.at[k, e],
                      plane_to(k, e))

    lwg[0] = jnp.zeros((8, 128), jnp.float32)
    cw.wait()
    lwg[0, 0:1, 0:per] = lwv[...]

    def turn(h):
        uvt[0, h] = uvb[pl.ds(pl.multiple_of(h * half, half), half), :].T

    cu.wait()
    turn(core)
    pl.semaphore_wait(barrier, n_z - 1 + len(plane))
    for s in range(PARTS):
        for e in range(1, n_y):
            uv_copy(e, s).start()
    for d in range(1, n_z):
        lw_copy(d).start()
    for e in range(1, n_y):
        pos_copy(e).start()

    cx.wait()
    hidden = None
    for c in range(CHUNKS):
        c1[c].wait()
        part = jnp.dot(xv[:, c * deep:(c + 1) * deep], w1v[c * deep:(c + 1) * deep, :],
                       preferred_element_type=jnp.float32)
        hidden = part if c == 0 else hidden + part
    hidden = jnp.maximum(hidden, 0.0).astype(jnp.bfloat16)
    c2.wait()
    emb[0] = jnp.dot(hidden, w2v[...], preferred_element_type=jnp.float32).astype(jnp.bfloat16)
    for d in range(1, n_z):
        emb_copy(d).start()
    turn(1 - core)

    eye = (lax.broadcasted_iota(jnp.int32, (per, 128), 0)
           == lax.broadcasted_iota(jnp.int32, (per, 128), 1))
    item_of = lax.broadcasted_iota(jnp.int32, (per, half), 0)

    def block(d, e, slot, h, carry):
        row_max, row_sum, row_pos = carry
        scores = jnp.dot(emb[d], uvt[e, h], preferred_element_type=jnp.float32) * inverse_temp
        top = jnp.max(scores, axis=1, keepdims=True)
        lse = top + jnp.log(jnp.sum(jnp.exp(scores - top), axis=1, keepdims=True))
        row = 2 * e + slot
        col_part[d, row:row + 1, :] = jnp.sum(jnp.where(eye, lse, 0.0), axis=0, keepdims=True)
        weight = jnp.sum(jnp.where(eye, lwg[d, 0:1, :], 0.0), axis=1, keepdims=True)
        logits = scores + weight
        new_max = jnp.maximum(row_max, jnp.max(logits, axis=0, keepdims=True))
        row_sum = row_sum * jnp.exp(row_max - new_max) + jnp.sum(
            jnp.exp(logits - new_max), axis=0, keepdims=True)
        start = (i * n_user + lax.rem(z + n_z - d, n_z) * n_y + y) * per
        hits = posb[e, h] == start + item_of
        row_pos = row_pos + jnp.sum(jnp.where(hits, logits, 0.0), axis=0, keepdims=True)
        return new_max, row_sum, row_pos

    def joined(parts):
        top = jnp.max(parts, axis=0, keepdims=True)
        return top + jnp.log(jnp.sum(jnp.exp(parts - top), axis=0, keepdims=True))

    def col_stats(d):
        return jnp.broadcast_to(joined(col_part[d, 0:2 * n_y, :]), (8, 128))

    def send_col(d):
        col_send[d] = col_stats(d)
        col_copy(d).start()

    def loop(low, high, step, carry):
        if n_z <= 4:
            for d in range(low, high):
                carry = step(d, carry)
            return carry
        return lax.fori_loop(low, high, step, carry)

    empty = (jnp.full((1, half), -1e30, jnp.float32), jnp.zeros((1, half), jnp.float32),
             jnp.zeros((1, half), jnp.float32))

    def own_block(d, carry):
        return tuple(block(d, 0, h, h, carry[h]) for h in range(2))

    def own_step(d, carry):
        lw_copy(d).wait_recv()
        emb_copy(d).wait_recv()
        return own_block(d, carry)

    halves = (core, 1 - core)
    last = n_z - 1
    cp.wait()
    own = own_block(0, (empty, empty))
    for s in range(PARTS):
        for e in range(1, n_y):
            uv_copy(e, s).wait_recv()
            uv_share(e, s).start()
        if s == 0:
            own = loop(1, min(2, last), own_step, own)
    others = []
    for e in range(1, n_y):
        pos_copy(e).wait_recv()
        others.append([loop(0, min(2, last), lambda d, carry, e=e: block(d, e, 0, halves[0], carry), empty)])
    own = loop(min(2, last), last, own_step, own)
    for e in range(1, n_y):
        for s in range(PARTS):
            uv_share(e, s).wait_recv()
    for e in range(1, n_y):
        first = others[e - 1][0]
        others[e - 1] = [
            loop(min(2, last), last, lambda d, carry, e=e: block(d, e, 0, halves[0], carry), first),
            loop(0, last, lambda d, carry, e=e: block(d, e, 1, halves[1], carry), empty)]

    def send_step(d, carry):
        send_col(d)
        return carry

    loop(1, last, send_step, 0)
    if last > 0:
        own = own_step(last, own)
        others = [[block(last, e, k, halves[k], others[e - 1][k]) for k in range(2)]
                  for e in range(1, n_y)]
        send_col(last)
    col_recv[0] = col_stats(0)

    for e, carry in enumerate([own] + others):
        stats = [(row_max + jnp.log(row_sum), row_pos) for row_max, row_sum, row_pos in carry]
        if e > 0:
            low = [jnp.where(core == 0, a, b) for a, b in zip(*stats)]
            high = [jnp.where(core == 0, b, a) for a, b in zip(*stats)]
            stats = [low, high]
        row_send[(n_y - e) % n_y] = jnp.concatenate(
            [stats[h][m][:, 128 * k:128 * (k + 1)] for m in range(2) for h in range(2)
             for k in range(rows // 2)], axis=0)
    for k, e in plane:
        row_copy(k, e).start()
    row_recv[0, 0] = row_send[0]

    for d in range(1, n_z):
        col_copy(d).wait_recv()
    col_ref[...] = joined(col_recv[:, 0, :])[:, 0:per]

    for k, e in plane:
        row_copy(k, e).wait_recv()
    stats = row_recv[...].reshape(n_item * n_y, 2 * rows, 128)
    lse_all = stats[:, 0:rows, :]
    top = jnp.max(lse_all, axis=0)
    total = top + jnp.log(jnp.sum(jnp.exp(lse_all - top), axis=0))
    row_ref[...] = total - jnp.sum(stats[:, rows:2 * rows, :], axis=0)

    for d in range(1, n_z):
        lw_copy(d).wait_send()
        emb_copy(d).wait_send()
        col_copy(d).wait_send()
    for e in range(1, n_y):
        pos_copy(e).wait_send()
        for s in range(PARTS):
            uv_copy(e, s).wait_send()
            uv_share(e, s).wait_send()
    for k, e in plane:
        row_copy(k, e).wait_send()


def hand_out(row_in, col_in, row_out, col_out, sem):
    first = pltpu.make_async_copy(row_in, row_out, sem.at[0])
    second = pltpu.make_async_copy(col_in, col_out, sem.at[1])
    first.start()
    second.start()
    first.wait()
    second.wait()


def on_device(n_user, n_item, n_y, item_features, layer_one, layer_two, log_weight, user_vectors,
              positive_index):
    per, d_in = item_features.shape
    d_hid, d_emb = layer_two.shape
    users = user_vectors.shape[0]
    n_z = n_user // n_y
    rows = users // 128
    anywhere = pl.BlockSpec(memory_space=pltpu.HBM)
    vmem = pl.BlockSpec(memory_space=pltpu.VMEM)
    dma = pltpu.SemaphoreType.DMA
    shapes = (jax.ShapeDtypeStruct((rows, 128), jnp.float32),
              jax.ShapeDtypeStruct((1, per), jnp.float32))
    row, col = pl.pallas_call(
        functools.partial(kernel, n_user, n_item, n_y),
        out_shape=(pltpu.VMEM((rows, 128), jnp.float32), pltpu.VMEM((1, per), jnp.float32)),
        in_specs=[anywhere] * 6,
        out_specs=(vmem, vmem),
        scratch_shapes=[
            pltpu.VMEM((per, d_in), jnp.bfloat16),
            pltpu.VMEM((d_in, d_hid), jnp.bfloat16),
            pltpu.VMEM((d_hid, d_emb), jnp.bfloat16),
            pltpu.VMEM((users, d_emb), jnp.bfloat16),
            pltpu.VMEM((n_y, 2, d_emb, users // 2), jnp.bfloat16),
            pltpu.VMEM((n_y, 2, 1, users // 2), jnp.int32),
            pltpu.VMEM((1, per), jnp.float32),
            pltpu.VMEM((n_z, per, d_emb), jnp.bfloat16),
            pltpu.VMEM((n_z, 8, 128), jnp.float32),
            pltpu.VMEM((n_z, 8, 128), jnp.float32),
            pltpu.VMEM((n_z, 8, 128), jnp.float32),
            pltpu.VMEM((n_z, 8, 128), jnp.float32),
            pltpu.VMEM((n_y, 2 * rows, 128), jnp.float32),
            pltpu.VMEM((n_item, n_y, 2 * rows, 128), jnp.float32),
            dma((5,)),
            dma((CHUNKS,)),
            dma((n_z,)),
            dma((n_z,)),
            dma((n_z,)),
            dma((n_z,)),
            dma((n_z,)),
            dma((n_z,)),
            dma((n_y, 2, PARTS)),
            dma((n_y, 2, PARTS)),
            dma((n_y,)),
            dma((n_y,)),
            dma((n_item, n_y)),
            dma((n_item, n_y)),
        ],
        compiler_params=pltpu.CompilerParams(
            collective_id=0, has_side_effects=True, vmem_limit_bytes=62 * 1024 * 1024),
    )(item_features, layer_one, layer_two, log_weight.reshape(1, per), user_vectors,
      positive_index.reshape(2, 1, users // 2))
    row, col = pl.pallas_call(
        hand_out,
        out_shape=shapes,
        in_specs=[pl.BlockSpec(memory_space=pl.ANY)] * 2,
        out_specs=(anywhere, anywhere),
        scratch_shapes=[dma((2,))],
        compiler_params=pltpu.CompilerParams(vmem_limit_bytes=4 * 1024 * 1024),
    )(row, col)
    return row.reshape(users), col.reshape(per)


def solution(mesh):
    n_user, n_item = mesh.shape["user"], mesh.shape["item"]
    n_y = 1
    while n_user % (2 * n_y) == 0 and 8 * n_y * n_y <= n_user:
        n_y *= 2
    placed = (P(("item", "user"), None), P(), P(), P(("item", "user")), P("user", None), P("user"))
    return jax.shard_map(
        functools.partial(on_device, n_user, n_item, n_y),
        mesh=mesh,
        in_specs=placed,
        out_specs=(P("user"), P(("item", "user"))),
        check_vma=False,
    )
```

```python
import functools
import math

import jax
import jax.numpy as jnp
from jax import lax
from jax.experimental import pallas as pl
from jax.experimental.pallas import tpu as pltpu
from jax.sharding import PartitionSpec as P

MESH = pl.DeviceIdType.MESH
CHUNKS = 4
PARTS = 2


def kernel(n_user, n_item, n_y, x_hbm, w1_hbm, w2_hbm, lw_hbm, uv_hbm, pos_hbm, row_ref, col_ref,
           xv, w1v, w2v, uvb, uvt, posb, lwv, emb, lwg, col_part, col_send, col_recv, row_send, row_recv,
           in_sem, w1_sem, lw_ssem, lw_rsem, emb_ssem, emb_rsem, col_ssem, col_rsem,
           uv_ssem, uv_rsem, pos_ssem, pos_rsem, row_ssem, row_rsem):
    n_z = n_user // n_y
    u = lax.axis_index("user")
    i = lax.axis_index("item")
    z, y = u // n_y, u % n_y
    core = lax.rem(i, 2)
    mate = i + 1 - 2 * core
    per = xv.shape[0]
    users, d_emb = uvb.shape
    half = users // 2
    sub = d_emb // PARTS
    rows = users // 128
    inverse_temp = 4.0 / math.sqrt(d_emb)
    deep = w1v.shape[0] // CHUNKS

    cu = pltpu.make_async_copy(uv_hbm, uvb, in_sem.at[2])
    cu.start()
    cx = pltpu.make_async_copy(x_hbm, xv, in_sem.at[0])
    cx.start()
    cw = pltpu.make_async_copy(lw_hbm, lwv, in_sem.at[4])
    cw.start()
    c1 = []
    for c in range(CHUNKS):
        part = pl.ds(c * deep, deep)
        c1.append(pltpu.make_async_copy(w1_hbm.at[part], w1v.at[part], w1_sem.at[c]))
        c1[-1].start()
    c2 = pltpu.make_async_copy(w2_hbm, w2v, in_sem.at[1])
    c2.start()
    cp = pltpu.make_async_copy(pos_hbm, posb.at[0], in_sem.at[3])
    cp.start()

    def other(k):
        place = 0
        for a in range(n_z):
            near = sorted((b for b in range(n_z) if b != a),
                          key=lambda b: (abs(b - a), abs(2 * b - n_z + 1)))
            here = 1 - ((z - a) * (z - a) + n_z * n_z - 1) // (n_z * n_z)
            place = place + near[k - 1] * here
        return place

    ordered = n_z <= 4
    ahead = [0] + [lax.rem(other(k) - z + n_z, n_z) if ordered else k for k in range(1, n_z)]
    behind = [0] + [lax.rem(z - other(k) + n_z, n_z) if ordered else k for k in range(1, n_z)]

    def slot(k):
        return behind[k] if ordered else k

    def z_to(d):
        return {"user": lax.rem(z + d, n_z) * n_y + y}

    def y_to(e):
        return {"user": z * n_y + lax.rem(y + e, n_y)}

    def plane_to(k, e):
        return {"user": z * n_y + lax.rem(y + e, n_y), "item": lax.rem(i + k, n_item)}

    plane = [(k, e) for e in range(n_y - 1, -1, -1) for k in range(n_item) if (k, e) != (0, 0)]

    barrier = pltpu.get_barrier_semaphore()
    for d in range(1, n_z):
        pl.semaphore_signal(barrier, inc=1, device_id=z_to(d), device_id_type=MESH)
    for k, e in plane:
        pl.semaphore_signal(barrier, inc=1, device_id=plane_to(k, e), device_id_type=MESH)

    def remote(src, dst, ssem, rsem, to):
        return pltpu.make_async_remote_copy(src_ref=src, dst_ref=dst, send_sem=ssem, recv_sem=rsem,
                                            device_id=to, device_id_type=MESH)

    def lw_copy(d):
        return remote(lwg.at[0], lwg.at[d], lw_ssem.at[d], lw_rsem.at[d], z_to(d))

    def emb_copy(d):
        return remote(emb.at[0], emb.at[d], emb_ssem.at[d], emb_rsem.at[d], z_to(d))

    def col_copy(d):
        return remote(col_send.at[d], col_recv.at[d], col_ssem.at[d], col_rsem.at[d], z_to(n_z - d))

    def uv_copy(e, s):
        part = pl.ds(s * sub, sub)
        return remote(uvt.at[0, core, part], uvt.at[e, core, part],
                      uv_ssem.at[e, 0, s], uv_rsem.at[e, 0, s], y_to(e))

    def uv_share(e, s):
        part = pl.ds(s * sub, sub)
        return remote(uvt.at[e, core, part], uvt.at[e, core, part],
                      uv_ssem.at[e, 1, s], uv_rsem.at[e, 1, s], {"item": mate})

    def pos_copy(e):
        return remote(pos_hbm, posb.at[e], pos_ssem.at[e], pos_rsem.at[e], y_to(e))

    def row_copy(k, e):
        return remote(row_send.at[e], row_recv.at[k, e], row_ssem.at[k, e], row_rsem.at[k, e],
                      plane_to(k, e))

    lwg[0] = jnp.zeros((8, 128), jnp.float32)
    cw.wait()
    lwg[0, 0:1, 0:per] = lwv[...]

    def turn(h):
        uvt[0, h] = uvb[pl.ds(pl.multiple_of(h * half, half), half), :].T

    cu.wait()
    turn(core)
    pl.semaphore_wait(barrier, n_z - 1 + len(plane))
    for s in range(PARTS):
        for e in range(1, n_y):
            uv_copy(e, s).start()
    for d in range(1, n_z):
        lw_copy(d).start()
    for e in range(1, n_y):
        pos_copy(e).start()

    cx.wait()
    hidden = None
    for c in range(CHUNKS):
        c1[c].wait()
        part = jnp.dot(xv[:, c * deep:(c + 1) * deep], w1v[c * deep:(c + 1) * deep, :],
                       preferred_element_type=jnp.float32)
        hidden = part if c == 0 else hidden + part
    hidden = jnp.maximum(hidden, 0.0).astype(jnp.bfloat16)
    c2.wait()
    emb[0] = jnp.dot(hidden, w2v[...], preferred_element_type=jnp.float32).astype(jnp.bfloat16)
    for k in range(1, n_z):
        emb_copy(ahead[k]).start()
    turn(1 - core)

    eye = (lax.broadcasted_iota(jnp.int32, (per, 128), 0)
           == lax.broadcasted_iota(jnp.int32, (per, 128), 1))
    item_of = lax.broadcasted_iota(jnp.int32, (per, half), 0)

    def block(d, e, side, h, carry):
        row_max, row_sum, row_pos = carry
        scores = jnp.dot(emb[d], uvt[e, h], preferred_element_type=jnp.float32) * inverse_temp
        top = jnp.max(scores, axis=1, keepdims=True)
        lse = top + jnp.log(jnp.sum(jnp.exp(scores - top), axis=1, keepdims=True))
        row = 2 * e + side
        col_part[d, row:row + 1, :] = jnp.sum(jnp.where(eye, lse, 0.0), axis=0, keepdims=True)
        weight = jnp.sum(jnp.where(eye, lwg[d, 0:1, :], 0.0), axis=1, keepdims=True)
        logits = scores + weight
        new_max = jnp.maximum(row_max, jnp.max(logits, axis=0, keepdims=True))
        row_sum = row_sum * jnp.exp(row_max - new_max) + jnp.sum(
            jnp.exp(logits - new_max), axis=0, keepdims=True)
        start = (i * n_user + lax.rem(z + n_z - d, n_z) * n_y + y) * per
        hits = posb[e, h] == start + item_of
        row_pos = row_pos + jnp.sum(jnp.where(hits, logits, 0.0), axis=0, keepdims=True)
        return new_max, row_sum, row_pos

    def joined(parts):
        top = jnp.max(parts, axis=0, keepdims=True)
        return top + jnp.log(jnp.sum(jnp.exp(parts - top), axis=0, keepdims=True))

    def col_stats(d):
        return jnp.broadcast_to(joined(col_part[d, 0:2 * n_y, :]), (8, 128))

    def send_col(d):
        col_send[d] = col_stats(d)
        col_copy(d).start()

    def loop(low, high, step, carry):
        if n_z <= 4:
            for d in range(low, high):
                carry = step(d, carry)
            return carry
        return lax.fori_loop(low, high, step, carry)

    empty = (jnp.full((1, half), -1e30, jnp.float32), jnp.zeros((1, half), jnp.float32),
             jnp.zeros((1, half), jnp.float32))

    def own_block(d, carry):
        return tuple(block(d, 0, h, h, carry[h]) for h in range(2))

    def own_step(k, carry):
        d = slot(k)
        lw_copy(d).wait_recv()
        emb_copy(d).wait_recv()
        return own_block(d, carry)

    halves = (core, 1 - core)
    last = n_z - 1
    cp.wait()
    own = own_block(0, (empty, empty))
    for s in range(PARTS):
        for e in range(1, n_y):
            uv_copy(e, s).wait_recv()
            uv_share(e, s).start()
        if s == 0:
            own = loop(1, min(2, last), own_step, own)
    others = []
    for e in range(1, n_y):
        pos_copy(e).wait_recv()
        others.append([loop(0, min(2, last), lambda k, carry, e=e: block(slot(k), e, 0, halves[0], carry), empty)])
    own = loop(min(2, last), last, own_step, own)
    for e in range(1, n_y):
        for s in range(PARTS):
            uv_share(e, s).wait_recv()
    for e in range(1, n_y):
        first = others[e - 1][0]
        others[e - 1] = [
            loop(min(2, last), last, lambda k, carry, e=e: block(slot(k), e, 0, halves[0], carry), first),
            loop(0, last, lambda k, carry, e=e: block(slot(k), e, 1, halves[1], carry), empty)]

    def send_step(k, carry):
        send_col(slot(k))
        return carry

    loop(1, last, send_step, 0)
    if last > 0:
        own = own_step(last, own)
        others = [[block(slot(last), e, k, halves[k], others[e - 1][k]) for k in range(2)]
                  for e in range(1, n_y)]
        send_col(slot(last))
    col_recv[0] = col_stats(0)

    for e, carry in enumerate([own] + others):
        stats = [(row_max + jnp.log(row_sum), row_pos) for row_max, row_sum, row_pos in carry]
        if e > 0:
            low = [jnp.where(core == 0, a, b) for a, b in zip(*stats)]
            high = [jnp.where(core == 0, b, a) for a, b in zip(*stats)]
            stats = [low, high]
        row_send[(n_y - e) % n_y] = jnp.concatenate(
            [stats[h][m][:, 128 * k:128 * (k + 1)] for m in range(2) for h in range(2)
             for k in range(rows // 2)], axis=0)
    for k, e in plane:
        row_copy(k, e).start()
    row_recv[0, 0] = row_send[0]

    for d in range(1, n_z):
        col_copy(d).wait_recv()
    col_ref[...] = joined(col_recv[:, 0, :])[:, 0:per]

    for k, e in plane:
        row_copy(k, e).wait_recv()
    stats = row_recv[...].reshape(n_item * n_y, 2 * rows, 128)
    lse_all = stats[:, 0:rows, :]
    top = jnp.max(lse_all, axis=0)
    total = top + jnp.log(jnp.sum(jnp.exp(lse_all - top), axis=0))
    row_ref[...] = total - jnp.sum(stats[:, rows:2 * rows, :], axis=0)

    for d in range(1, n_z):
        lw_copy(d).wait_send()
        emb_copy(d).wait_send()
        col_copy(d).wait_send()
    for e in range(1, n_y):
        pos_copy(e).wait_send()
        for s in range(PARTS):
            uv_copy(e, s).wait_send()
            uv_share(e, s).wait_send()
    for k, e in plane:
        row_copy(k, e).wait_send()


def hand_out(row_in, col_in, row_out, col_out, sem):
    first = pltpu.make_async_copy(row_in, row_out, sem.at[0])
    second = pltpu.make_async_copy(col_in, col_out, sem.at[1])
    first.start()
    second.start()
    first.wait()
    second.wait()


def on_device(n_user, n_item, n_y, item_features, layer_one, layer_two, log_weight, user_vectors,
              positive_index):
    per, d_in = item_features.shape
    d_hid, d_emb = layer_two.shape
    users = user_vectors.shape[0]
    n_z = n_user // n_y
    rows = users // 128
    anywhere = pl.BlockSpec(memory_space=pltpu.HBM)
    vmem = pl.BlockSpec(memory_space=pltpu.VMEM)
    dma = pltpu.SemaphoreType.DMA
    shapes = (jax.ShapeDtypeStruct((rows, 128), jnp.float32),
              jax.ShapeDtypeStruct((1, per), jnp.float32))
    row, col = pl.pallas_call(
        functools.partial(kernel, n_user, n_item, n_y),
        out_shape=(pltpu.VMEM((rows, 128), jnp.float32), pltpu.VMEM((1, per), jnp.float32)),
        in_specs=[anywhere] * 6,
        out_specs=(vmem, vmem),
        scratch_shapes=[
            pltpu.VMEM((per, d_in), jnp.bfloat16),
            pltpu.VMEM((d_in, d_hid), jnp.bfloat16),
            pltpu.VMEM((d_hid, d_emb), jnp.bfloat16),
            pltpu.VMEM((users, d_emb), jnp.bfloat16),
            pltpu.VMEM((n_y, 2, d_emb, users // 2), jnp.bfloat16),
            pltpu.VMEM((n_y, 2, 1, users // 2), jnp.int32),
            pltpu.VMEM((1, per), jnp.float32),
            pltpu.VMEM((n_z, per, d_emb), jnp.bfloat16),
            pltpu.VMEM((n_z, 8, 128), jnp.float32),
            pltpu.VMEM((n_z, 8, 128), jnp.float32),
            pltpu.VMEM((n_z, 8, 128), jnp.float32),
            pltpu.VMEM((n_z, 8, 128), jnp.float32),
            pltpu.VMEM((n_y, 2 * rows, 128), jnp.float32),
            pltpu.VMEM((n_item, n_y, 2 * rows, 128), jnp.float32),
            dma((5,)),
            dma((CHUNKS,)),
            dma((n_z,)),
            dma((n_z,)),
            dma((n_z,)),
            dma((n_z,)),
            dma((n_z,)),
            dma((n_z,)),
            dma((n_y, 2, PARTS)),
            dma((n_y, 2, PARTS)),
            dma((n_y,)),
            dma((n_y,)),
            dma((n_item, n_y)),
            dma((n_item, n_y)),
        ],
        compiler_params=pltpu.CompilerParams(
            collective_id=0, has_side_effects=True, vmem_limit_bytes=62 * 1024 * 1024),
    )(item_features, layer_one, layer_two, log_weight.reshape(1, per), user_vectors,
      positive_index.reshape(2, 1, users // 2))
    row, col = pl.pallas_call(
        hand_out,
        out_shape=shapes,
        in_specs=[pl.BlockSpec(memory_space=pl.ANY)] * 2,
        out_specs=(anywhere, anywhere),
        scratch_shapes=[dma((2,))],
        compiler_params=pltpu.CompilerParams(vmem_limit_bytes=4 * 1024 * 1024),
    )(row, col)
    return row.reshape(users), col.reshape(per)


def solution(mesh):
    n_user, n_item = mesh.shape["user"], mesh.shape["item"]
    n_y = 1
    while n_user % (2 * n_y) == 0 and 8 * n_y * n_y <= n_user:
        n_y *= 2
    placed = (P(("item", "user"), None), P(), P(), P(("item", "user")), P("user", None), P("user"))
    return jax.shard_map(
        functools.partial(on_device, n_user, n_item, n_y),
        mesh=mesh,
        in_specs=placed,
        out_specs=(P("user"), P(("item", "user"))),
        check_vma=False,
    )
```

```python
import functools
import math

import jax
import jax.numpy as jnp
from jax import lax
from jax.experimental import pallas as pl
from jax.experimental.pallas import tpu as pltpu
from jax.sharding import PartitionSpec as P

MESH = pl.DeviceIdType.MESH
CHUNKS = 4
PARTS = 2


def kernel(n_user, n_item, n_y, x_hbm, w1_hbm, w2_hbm, lw_hbm, uv_hbm, pos_hbm, row_ref, col_ref,
           xv, w1v, w2v, uvb, uvt, posb, lwv, emb, lwg, col_part, col_send, col_recv, row_send, row_recv,
           in_sem, w1_sem, lw_ssem, lw_rsem, emb_ssem, emb_rsem, col_ssem, col_rsem,
           uv_ssem, uv_rsem, pos_ssem, pos_rsem, row_ssem, row_rsem):
    n_z = n_user // n_y
    u = lax.axis_index("user")
    i = lax.axis_index("item")
    z, y = u // n_y, u % n_y
    core = lax.rem(i, 2)
    mate = i + 1 - 2 * core
    per = xv.shape[0]
    users, d_emb = uvb.shape
    half = users // 2
    sub = d_emb // PARTS
    rows = users // 128
    inverse_temp = 4.0 / math.sqrt(d_emb)
    deep = w1v.shape[0] // CHUNKS

    cu = pltpu.make_async_copy(uv_hbm, uvb, in_sem.at[2])
    cu.start()
    cx = pltpu.make_async_copy(x_hbm, xv, in_sem.at[0])
    cx.start()
    cw = pltpu.make_async_copy(lw_hbm, lwv, in_sem.at[4])
    cw.start()
    c1 = []
    for c in range(CHUNKS):
        part = pl.ds(c * deep, deep)
        c1.append(pltpu.make_async_copy(w1_hbm.at[part], w1v.at[part], w1_sem.at[c]))
        c1[-1].start()
    c2 = pltpu.make_async_copy(w2_hbm, w2v, in_sem.at[1])
    c2.start()
    cp = pltpu.make_async_copy(pos_hbm, posb.at[0], in_sem.at[3])
    cp.start()

    def z_to(d):
        return {"user": lax.rem(z + d, n_z) * n_y + y}

    def y_to(e):
        return {"user": z * n_y + lax.rem(y + e, n_y)}

    def plane_to(k, e):
        return {"user": z * n_y + lax.rem(y + e, n_y), "item": lax.rem(i + k, n_item)}

    plane = [(k, e) for e in range(n_y - 1, -1, -1) for k in range(n_item) if (k, e) != (0, 0)]

    barrier = pltpu.get_barrier_semaphore()
    for d in range(1, n_z):
        pl.semaphore_signal(barrier, inc=1, device_id=z_to(d), device_id_type=MESH)
    for k, e in plane:
        pl.semaphore_signal(barrier, inc=1, device_id=plane_to(k, e), device_id_type=MESH)

    def remote(src, dst, ssem, rsem, to):
        return pltpu.make_async_remote_copy(src_ref=src, dst_ref=dst, send_sem=ssem, recv_sem=rsem,
                                            device_id=to, device_id_type=MESH)

    def lw_copy(d):
        return remote(lwg.at[0], lwg.at[d], lw_ssem.at[d], lw_rsem.at[d], z_to(d))

    def emb_copy(d):
        return remote(emb.at[0], emb.at[d], emb_ssem.at[d], emb_rsem.at[d], z_to(d))

    def col_copy(d):
        return remote(col_send.at[d], col_recv.at[d], col_ssem.at[d], col_rsem.at[d], z_to(n_z - d))

    def uv_copy(e, s):
        part = pl.ds(s * sub, sub)
        return remote(uvt.at[0, core, part], uvt.at[e, core, part],
                      uv_ssem.at[e, 0, s], uv_rsem.at[e, 0, s], y_to(e))

    def uv_share(e, s):
        part = pl.ds(s * sub, sub)
        return remote(uvt.at[e, core, part], uvt.at[e, core, part],
                      uv_ssem.at[e, 1, s], uv_rsem.at[e, 1, s], {"item": mate})

    def pos_copy(e):
        return remote(pos_hbm, posb.at[e], pos_ssem.at[e], pos_rsem.at[e], y_to(e))

    def row_copy(k, e):
        return remote(row_send.at[e], row_recv.at[k, e], row_ssem.at[k, e], row_rsem.at[k, e],
                      plane_to(k, e))

    lwg[0] = jnp.zeros((8, 128), jnp.float32)
    cw.wait()
    lwg[0, 0:1, 0:per] = lwv[...]

    def turn(h):
        uvt[0, h] = uvb[pl.ds(pl.multiple_of(h * half, half), half), :].T

    cu.wait()
    turn(core)
    pl.semaphore_wait(barrier, n_z - 1 + len(plane))
    for s in range(PARTS):
        for e in range(1, n_y):
            uv_copy(e, s).start()
    for d in range(1, n_z):
        lw_copy(d).start()
    for e in range(1, n_y):
        pos_copy(e).start()

    cx.wait()
    hidden = None
    for c in range(CHUNKS):
        c1[c].wait()
        part = jnp.dot(xv[:, c * deep:(c + 1) * deep], w1v[c * deep:(c + 1) * deep, :],
                       preferred_element_type=jnp.float32)
        hidden = part if c == 0 else hidden + part
    hidden = jnp.maximum(hidden, 0.0).astype(jnp.bfloat16)
    c2.wait()
    emb[0] = jnp.dot(hidden, w2v[...], preferred_element_type=jnp.float32).astype(jnp.bfloat16)
    for d in range(1, n_z):
        emb_copy(d).start()
    turn(1 - core)

    eye = (lax.broadcasted_iota(jnp.int32, (per, 128), 0)
           == lax.broadcasted_iota(jnp.int32, (per, 128), 1))
    item_of = lax.broadcasted_iota(jnp.int32, (per, half), 0)

    def block(d, e, slot, h, carry, scores=None):
        row_max, row_sum, row_pos = carry
        if scores is None:
            scores = jnp.dot(emb[d], uvt[e, h], preferred_element_type=jnp.float32)
        scores = scores * inverse_temp
        top = jnp.max(scores, axis=1, keepdims=True)
        lse = top + jnp.log(jnp.sum(jnp.exp(scores - top), axis=1, keepdims=True))
        row = 2 * e + slot
        col_part[d, row:row + 1, :] = jnp.sum(jnp.where(eye, lse, 0.0), axis=0, keepdims=True)
        weight = jnp.sum(jnp.where(eye, lwg[d, 0:1, :], 0.0), axis=1, keepdims=True)
        logits = scores + weight
        new_max = jnp.maximum(row_max, jnp.max(logits, axis=0, keepdims=True))
        row_sum = row_sum * jnp.exp(row_max - new_max) + jnp.sum(
            jnp.exp(logits - new_max), axis=0, keepdims=True)
        start = (i * n_user + lax.rem(z + n_z - d, n_z) * n_y + y) * per
        hits = posb[e, h] == start + item_of
        row_pos = row_pos + jnp.sum(jnp.where(hits, logits, 0.0), axis=0, keepdims=True)
        return new_max, row_sum, row_pos

    def joined(parts):
        top = jnp.max(parts, axis=0, keepdims=True)
        return top + jnp.log(jnp.sum(jnp.exp(parts - top), axis=0, keepdims=True))

    def col_stats(d):
        return jnp.broadcast_to(joined(col_part[d, 0:2 * n_y, :]), (8, 128))

    def send_col(d):
        col_send[d] = col_stats(d)
        col_copy(d).start()

    def loop(low, high, step, carry):
        if n_z <= 4:
            for d in range(low, high):
                carry = step(d, carry)
            return carry
        return lax.fori_loop(low, high, step, carry)

    empty = (jnp.full((1, half), -1e30, jnp.float32), jnp.zeros((1, half), jnp.float32),
             jnp.zeros((1, half), jnp.float32))

    def own_block(d, carry):
        return tuple(block(d, 0, h, h, carry[h]) for h in range(2))

    def own_step(d, carry):
        lw_copy(d).wait_recv()
        emb_copy(d).wait_recv()
        return own_block(d, carry)

    halves = (core, 1 - core)
    cp.wait()
    own = own_block(0, (empty, empty))
    for s in range(PARTS):
        for e in range(1, n_y):
            uv_copy(e, s).wait_recv()
            uv_share(e, s).start()
    early = min(2, n_z)
    for d in range(1, early):
        own = own_step(d, own)
    for e in range(1, n_y):
        pos_copy(e).wait_recv()
        for s in range(PARTS):
            uv_share(e, s).wait_recv()

    rows_here = emb[0:early].reshape(early * per, d_emb)
    others = []
    for e in range(1, n_y):
        pair = []
        for k in range(2):
            scores = jnp.dot(rows_here, uvt[e, halves[k]], preferred_element_type=jnp.float32)
            carry = empty
            for d in range(early):
                carry = block(d, e, k, halves[k], carry, scores[d * per:(d + 1) * per])
            pair.append(carry)
        others.append(tuple(pair))
    for d in range(1, early):
        send_col(d)

    def full_step(d, carry):
        own, others = carry
        own = own_step(d, own)
        others = tuple(tuple(block(d, e, k, halves[k], others[e - 1][k]) for k in range(2))
                       for e in range(1, n_y))
        send_col(d)
        return own, others

    own, others = loop(early, n_z, full_step, (own, tuple(others)))
    others = list(others)
    col_recv[0] = col_stats(0)

    for e, carry in enumerate([own] + others):
        stats = [(row_max + jnp.log(row_sum), row_pos) for row_max, row_sum, row_pos in carry]
        if e > 0:
            low = [jnp.where(core == 0, a, b) for a, b in zip(*stats)]
            high = [jnp.where(core == 0, b, a) for a, b in zip(*stats)]
            stats = [low, high]
        row_send[(n_y - e) % n_y] = jnp.concatenate(
            [stats[h][m][:, 128 * k:128 * (k + 1)] for m in range(2) for h in range(2)
             for k in range(rows // 2)], axis=0)
    for k, e in plane:
        row_copy(k, e).start()
    row_recv[0, 0] = row_send[0]

    for d in range(1, n_z):
        col_copy(d).wait_recv()
    col_ref[...] = joined(col_recv[:, 0, :])[:, 0:per]

    for k, e in plane:
        row_copy(k, e).wait_recv()
    stats = row_recv[...].reshape(n_item * n_y, 2 * rows, 128)
    lse_all = stats[:, 0:rows, :]
    top = jnp.max(lse_all, axis=0)
    total = top + jnp.log(jnp.sum(jnp.exp(lse_all - top), axis=0))
    row_ref[...] = total - jnp.sum(stats[:, rows:2 * rows, :], axis=0)

    for d in range(1, n_z):
        lw_copy(d).wait_send()
        emb_copy(d).wait_send()
        col_copy(d).wait_send()
    for e in range(1, n_y):
        pos_copy(e).wait_send()
        for s in range(PARTS):
            uv_copy(e, s).wait_send()
            uv_share(e, s).wait_send()
    for k, e in plane:
        row_copy(k, e).wait_send()


def hand_out(row_in, col_in, row_out, col_out, sem):
    first = pltpu.make_async_copy(row_in, row_out, sem.at[0])
    second = pltpu.make_async_copy(col_in, col_out, sem.at[1])
    first.start()
    second.start()
    first.wait()
    second.wait()


def on_device(n_user, n_item, n_y, item_features, layer_one, layer_two, log_weight, user_vectors,
              positive_index):
    per, d_in = item_features.shape
    d_hid, d_emb = layer_two.shape
    users = user_vectors.shape[0]
    n_z = n_user // n_y
    rows = users // 128
    anywhere = pl.BlockSpec(memory_space=pltpu.HBM)
    vmem = pl.BlockSpec(memory_space=pltpu.VMEM)
    dma = pltpu.SemaphoreType.DMA
    shapes = (jax.ShapeDtypeStruct((rows, 128), jnp.float32),
              jax.ShapeDtypeStruct((1, per), jnp.float32))
    row, col = pl.pallas_call(
        functools.partial(kernel, n_user, n_item, n_y),
        out_shape=(pltpu.VMEM((rows, 128), jnp.float32), pltpu.VMEM((1, per), jnp.float32)),
        in_specs=[anywhere] * 6,
        out_specs=(vmem, vmem),
        scratch_shapes=[
            pltpu.VMEM((per, d_in), jnp.bfloat16),
            pltpu.VMEM((d_in, d_hid), jnp.bfloat16),
            pltpu.VMEM((d_hid, d_emb), jnp.bfloat16),
            pltpu.VMEM((users, d_emb), jnp.bfloat16),
            pltpu.VMEM((n_y, 2, d_emb, users // 2), jnp.bfloat16),
            pltpu.VMEM((n_y, 2, 1, users // 2), jnp.int32),
            pltpu.VMEM((1, per), jnp.float32),
            pltpu.VMEM((n_z, per, d_emb), jnp.bfloat16),
            pltpu.VMEM((n_z, 8, 128), jnp.float32),
            pltpu.VMEM((n_z, 8, 128), jnp.float32),
            pltpu.VMEM((n_z, 8, 128), jnp.float32),
            pltpu.VMEM((n_z, 8, 128), jnp.float32),
            pltpu.VMEM((n_y, 2 * rows, 128), jnp.float32),
            pltpu.VMEM((n_item, n_y, 2 * rows, 128), jnp.float32),
            dma((5,)),
            dma((CHUNKS,)),
            dma((n_z,)),
            dma((n_z,)),
            dma((n_z,)),
            dma((n_z,)),
            dma((n_z,)),
            dma((n_z,)),
            dma((n_y, 2, PARTS)),
            dma((n_y, 2, PARTS)),
            dma((n_y,)),
            dma((n_y,)),
            dma((n_item, n_y)),
            dma((n_item, n_y)),
        ],
        compiler_params=pltpu.CompilerParams(
            collective_id=0, has_side_effects=True, vmem_limit_bytes=62 * 1024 * 1024),
    )(item_features, layer_one, layer_two, log_weight.reshape(1, per), user_vectors,
      positive_index.reshape(2, 1, users // 2))
    row, col = pl.pallas_call(
        hand_out,
        out_shape=shapes,
        in_specs=[pl.BlockSpec(memory_space=pl.ANY)] * 2,
        out_specs=(anywhere, anywhere),
        scratch_shapes=[dma((2,))],
        compiler_params=pltpu.CompilerParams(vmem_limit_bytes=4 * 1024 * 1024),
    )(row, col)
    return row.reshape(users), col.reshape(per)


def solution(mesh):
    n_user, n_item = mesh.shape["user"], mesh.shape["item"]
    n_y = 1
    while n_user % (2 * n_y) == 0 and 8 * n_y * n_y <= n_user:
        n_y *= 2
    placed = (P(("item", "user"), None), P(), P(), P(("item", "user")), P("user", None), P("user"))
    return jax.shard_map(
        functools.partial(on_device, n_user, n_item, n_y),
        mesh=mesh,
        in_specs=placed,
        out_specs=(P("user"), P(("item", "user"))),
        check_vma=False,
    )
```

```python
import functools
import math

import jax
import jax.numpy as jnp
from jax import lax
from jax.experimental import pallas as pl
from jax.experimental.pallas import tpu as pltpu
from jax.sharding import PartitionSpec as P

MESH = pl.DeviceIdType.MESH
CHUNKS = 4
PARTS = 2


def kernel(n_user, n_item, n_y, x_hbm, w1_hbm, w2_hbm, lw_hbm, uv_hbm, pos_hbm, row_ref, col_ref,
           xv, w1v, w2v, uvb, uvt, posb, lwv, emb, lwg, col_part, col_send, col_recv, row_send, row_recv,
           in_sem, w1_sem, lw_ssem, lw_rsem, emb_ssem, emb_rsem, col_ssem, col_rsem,
           uv_ssem, uv_rsem, pos_ssem, pos_rsem, row_ssem, row_rsem):
    n_z = n_user // n_y
    u = lax.axis_index("user")
    i = lax.axis_index("item")
    z, y = u // n_y, u % n_y
    core = lax.rem(i, 2)
    mate = i + 1 - 2 * core
    per = xv.shape[0]
    users, d_emb = uvb.shape
    half = users // 2
    sub = d_emb // PARTS
    rows = users // 128
    inverse_temp = 4.0 / math.sqrt(d_emb)
    deep = w1v.shape[0] // CHUNKS

    cu = pltpu.make_async_copy(uv_hbm, uvb, in_sem.at[2])
    cu.start()
    cx = pltpu.make_async_copy(x_hbm, xv, in_sem.at[0])
    cx.start()
    cw = pltpu.make_async_copy(lw_hbm, lwv, in_sem.at[4])
    cw.start()
    c1 = []
    for c in range(CHUNKS):
        part = pl.ds(c * deep, deep)
        c1.append(pltpu.make_async_copy(w1_hbm.at[part], w1v.at[part], w1_sem.at[c]))
        c1[-1].start()
    c2 = pltpu.make_async_copy(w2_hbm, w2v, in_sem.at[1])
    c2.start()
    cp = pltpu.make_async_copy(pos_hbm, posb.at[0], in_sem.at[3])
    cp.start()

    def z_to(d):
        return {"user": lax.rem(z + d, n_z) * n_y + y}

    def y_to(e):
        return {"user": z * n_y + lax.rem(y + e, n_y)}

    def plane_to(k, e):
        return {"user": z * n_y + lax.rem(y + e, n_y), "item": lax.rem(i + k, n_item)}

    plane = [(k, e) for e in range(n_y - 1, -1, -1) for k in range(n_item) if (k, e) != (0, 0)]

    barrier = pltpu.get_barrier_semaphore()
    for d in range(1, n_z):
        pl.semaphore_signal(barrier, inc=1, device_id=z_to(d), device_id_type=MESH)
    for k, e in plane:
        pl.semaphore_signal(barrier, inc=1, device_id=plane_to(k, e), device_id_type=MESH)

    def remote(src, dst, ssem, rsem, to):
        return pltpu.make_async_remote_copy(src_ref=src, dst_ref=dst, send_sem=ssem, recv_sem=rsem,
                                            device_id=to, device_id_type=MESH)

    def lw_copy(d):
        return remote(lwg.at[0], lwg.at[d], lw_ssem.at[d], lw_rsem.at[d], z_to(d))

    def emb_copy(d):
        return remote(emb.at[0], emb.at[d], emb_ssem.at[d], emb_rsem.at[d], z_to(d))

    def col_copy(d):
        return remote(col_send.at[d], col_recv.at[d], col_ssem.at[d], col_rsem.at[d], z_to(n_z - d))

    def uv_copy(e, s):
        part = pl.ds(s * sub, sub)
        return remote(uvt.at[0, core, part], uvt.at[e, core, part],
                      uv_ssem.at[e, 0, s], uv_rsem.at[e, 0, s], y_to(e))

    def uv_share(e, s):
        part = pl.ds(s * sub, sub)
        return remote(uvt.at[e, core, part], uvt.at[e, core, part],
                      uv_ssem.at[e, 1, s], uv_rsem.at[e, 1, s], {"item": mate})

    def pos_copy(e):
        return remote(pos_hbm, posb.at[e], pos_ssem.at[e], pos_rsem.at[e], y_to(e))

    def row_copy(k, e):
        return remote(row_send.at[e], row_recv.at[k, e], row_ssem.at[k, e], row_rsem.at[k, e],
                      plane_to(k, e))

    lwg[0] = jnp.zeros((8, 128), jnp.float32)
    cw.wait()
    lwg[0, 0:1, 0:per] = lwv[...]

    def turn(h):
        uvt[0, h] = uvb[pl.ds(pl.multiple_of(h * half, half), half), :].T

    cu.wait()
    turn(core)
    pl.semaphore_wait(barrier, n_z - 1 + len(plane))
    for s in range(PARTS):
        for e in range(1, n_y):
            uv_copy(e, s).start()
    for d in range(1, n_z):
        lw_copy(d).start()
    for e in range(1, n_y):
        pos_copy(e).start()

    cx.wait()
    hidden = None
    for c in range(CHUNKS):
        c1[c].wait()
        part = jnp.dot(xv[:, c * deep:(c + 1) * deep], w1v[c * deep:(c + 1) * deep, :],
                       preferred_element_type=jnp.float32)
        hidden = part if c == 0 else hidden + part
    hidden = jnp.maximum(hidden, 0.0).astype(jnp.bfloat16)
    c2.wait()
    emb[0] = jnp.dot(hidden, w2v[...], preferred_element_type=jnp.float32).astype(jnp.bfloat16)
    for d in range(1, n_z):
        emb_copy(d).start()
    turn(1 - core)

    eye = (lax.broadcasted_iota(jnp.int32, (per, 128), 0)
           == lax.broadcasted_iota(jnp.int32, (per, 128), 1))
    item_of = lax.broadcasted_iota(jnp.int32, (per, half), 0)

    def block(d, e, slot, h, carry, scores=None):
        row_max, row_sum, row_pos = carry
        if scores is None:
            scores = jnp.dot(emb[d], uvt[e, h], preferred_element_type=jnp.float32)
        scores = scores * inverse_temp
        top = jnp.max(scores, axis=1, keepdims=True)
        lse = top + jnp.log(jnp.sum(jnp.exp(scores - top), axis=1, keepdims=True))
        row = 2 * e + slot
        col_part[d, row:row + 1, :] = jnp.sum(jnp.where(eye, lse, 0.0), axis=0, keepdims=True)
        weight = jnp.sum(jnp.where(eye, lwg[d, 0:1, :], 0.0), axis=1, keepdims=True)
        logits = scores + weight
        new_max = jnp.maximum(row_max, jnp.max(logits, axis=0, keepdims=True))
        row_sum = row_sum * jnp.exp(row_max - new_max) + jnp.sum(
            jnp.exp(logits - new_max), axis=0, keepdims=True)
        start = (i * n_user + lax.rem(z + n_z - d, n_z) * n_y + y) * per
        hits = posb[e, h] == start + item_of
        row_pos = row_pos + jnp.sum(jnp.where(hits, logits, 0.0), axis=0, keepdims=True)
        return new_max, row_sum, row_pos

    def joined(parts):
        top = jnp.max(parts, axis=0, keepdims=True)
        return top + jnp.log(jnp.sum(jnp.exp(parts - top), axis=0, keepdims=True))

    def col_stats(d):
        return jnp.broadcast_to(joined(col_part[d, 0:2 * n_y, :]), (8, 128))

    def send_col(d):
        col_send[d] = col_stats(d)
        col_copy(d).start()

    def loop(low, high, step, carry):
        if n_z <= 4:
            for d in range(low, high):
                carry = step(d, carry)
            return carry
        return lax.fori_loop(low, high, step, carry)

    empty = (jnp.full((1, half), -1e30, jnp.float32), jnp.zeros((1, half), jnp.float32),
             jnp.zeros((1, half), jnp.float32))

    def own_block(d, carry):
        return tuple(block(d, 0, h, h, carry[h]) for h in range(2))

    def own_step(d, carry):
        lw_copy(d).wait_recv()
        emb_copy(d).wait_recv()
        return own_block(d, carry)

    halves = (core, 1 - core)
    cp.wait()
    own = own_block(0, (empty, empty))
    for s in range(PARTS):
        for e in range(1, n_y):
            uv_copy(e, s).wait_recv()
            uv_share(e, s).start()
    early = 2 if n_z % 2 == 0 else 1
    for d in range(1, early):
        own = own_step(d, own)
    for e in range(1, n_y):
        pos_copy(e).wait_recv()
        for s in range(PARTS):
            uv_share(e, s).wait_recv()

    rows_here = emb[0:early].reshape(early * per, d_emb)
    others = []
    for e in range(1, n_y):
        pair = []
        for k in range(2):
            scores = jnp.dot(rows_here, uvt[e, halves[k]], preferred_element_type=jnp.float32)
            carry = empty
            for d in range(early):
                carry = block(d, e, k, halves[k], carry, scores[d * per:(d + 1) * per])
            pair.append(carry)
        others.append(tuple(pair))
    for d in range(1, early):
        send_col(d)

    def full_step(j, carry):
        own, others = carry
        group = [j * early + k for k in range(early)]
        for d in group:
            lw_copy(d).wait_recv()
            emb_copy(d).wait_recv()
        rows_now = emb[pl.ds(j * early, early)].reshape(early * per, d_emb)

        def meet(e, slot, h, carry):
            scores = jnp.dot(rows_now, uvt[e, h], preferred_element_type=jnp.float32)
            for k, d in enumerate(group):
                carry = block(d, e, slot, h, carry, scores[k * per:(k + 1) * per])
            return carry

        others = tuple(tuple(meet(e, k, halves[k], others[e - 1][k]) for k in range(2))
                       for e in range(1, n_y))
        own = tuple(meet(0, h, h, own[h]) for h in range(2))
        for d in group:
            send_col(d)
        return own, others

    own, others = loop(1, n_z // early, full_step, (own, tuple(others)))
    others = list(others)
    col_recv[0] = col_stats(0)

    for e, carry in enumerate([own] + others):
        stats = [(row_max + jnp.log(row_sum), row_pos) for row_max, row_sum, row_pos in carry]
        if e > 0:
            low = [jnp.where(core == 0, a, b) for a, b in zip(*stats)]
            high = [jnp.where(core == 0, b, a) for a, b in zip(*stats)]
            stats = [low, high]
        row_send[(n_y - e) % n_y] = jnp.concatenate(
            [stats[h][m][:, 128 * k:128 * (k + 1)] for m in range(2) for h in range(2)
             for k in range(rows // 2)], axis=0)
    for k, e in plane:
        row_copy(k, e).start()
    row_recv[0, 0] = row_send[0]

    for d in range(1, n_z):
        col_copy(d).wait_recv()
    col_ref[...] = joined(col_recv[:, 0, :])[:, 0:per]

    for k, e in plane:
        row_copy(k, e).wait_recv()
    stats = row_recv[...].reshape(n_item * n_y, 2 * rows, 128)
    lse_all = stats[:, 0:rows, :]
    top = jnp.max(lse_all, axis=0)
    total = top + jnp.log(jnp.sum(jnp.exp(lse_all - top), axis=0))
    row_ref[...] = total - jnp.sum(stats[:, rows:2 * rows, :], axis=0)

    for d in range(1, n_z):
        lw_copy(d).wait_send()
        emb_copy(d).wait_send()
        col_copy(d).wait_send()
    for e in range(1, n_y):
        pos_copy(e).wait_send()
        for s in range(PARTS):
            uv_copy(e, s).wait_send()
            uv_share(e, s).wait_send()
    for k, e in plane:
        row_copy(k, e).wait_send()


def hand_out(row_in, col_in, row_out, col_out, sem):
    first = pltpu.make_async_copy(row_in, row_out, sem.at[0])
    second = pltpu.make_async_copy(col_in, col_out, sem.at[1])
    first.start()
    second.start()
    first.wait()
    second.wait()


def on_device(n_user, n_item, n_y, item_features, layer_one, layer_two, log_weight, user_vectors,
              positive_index):
    per, d_in = item_features.shape
    d_hid, d_emb = layer_two.shape
    users = user_vectors.shape[0]
    n_z = n_user // n_y
    rows = users // 128
    anywhere = pl.BlockSpec(memory_space=pltpu.HBM)
    vmem = pl.BlockSpec(memory_space=pltpu.VMEM)
    dma = pltpu.SemaphoreType.DMA
    shapes = (jax.ShapeDtypeStruct((rows, 128), jnp.float32),
              jax.ShapeDtypeStruct((1, per), jnp.float32))
    row, col = pl.pallas_call(
        functools.partial(kernel, n_user, n_item, n_y),
        out_shape=(pltpu.VMEM((rows, 128), jnp.float32), pltpu.VMEM((1, per), jnp.float32)),
        in_specs=[anywhere] * 6,
        out_specs=(vmem, vmem),
        scratch_shapes=[
            pltpu.VMEM((per, d_in), jnp.bfloat16),
            pltpu.VMEM((d_in, d_hid), jnp.bfloat16),
            pltpu.VMEM((d_hid, d_emb), jnp.bfloat16),
            pltpu.VMEM((users, d_emb), jnp.bfloat16),
            pltpu.VMEM((n_y, 2, d_emb, users // 2), jnp.bfloat16),
            pltpu.VMEM((n_y, 2, 1, users // 2), jnp.int32),
            pltpu.VMEM((1, per), jnp.float32),
            pltpu.VMEM((n_z, per, d_emb), jnp.bfloat16),
            pltpu.VMEM((n_z, 8, 128), jnp.float32),
            pltpu.VMEM((n_z, 8, 128), jnp.float32),
            pltpu.VMEM((n_z, 8, 128), jnp.float32),
            pltpu.VMEM((n_z, 8, 128), jnp.float32),
            pltpu.VMEM((n_y, 2 * rows, 128), jnp.float32),
            pltpu.VMEM((n_item, n_y, 2 * rows, 128), jnp.float32),
            dma((5,)),
            dma((CHUNKS,)),
            dma((n_z,)),
            dma((n_z,)),
            dma((n_z,)),
            dma((n_z,)),
            dma((n_z,)),
            dma((n_z,)),
            dma((n_y, 2, PARTS)),
            dma((n_y, 2, PARTS)),
            dma((n_y,)),
            dma((n_y,)),
            dma((n_item, n_y)),
            dma((n_item, n_y)),
        ],
        compiler_params=pltpu.CompilerParams(
            collective_id=0, has_side_effects=True, vmem_limit_bytes=62 * 1024 * 1024),
    )(item_features, layer_one, layer_two, log_weight.reshape(1, per), user_vectors,
      positive_index.reshape(2, 1, users // 2))
    row, col = pl.pallas_call(
        hand_out,
        out_shape=shapes,
        in_specs=[pl.BlockSpec(memory_space=pl.ANY)] * 2,
        out_specs=(anywhere, anywhere),
        scratch_shapes=[dma((2,))],
        compiler_params=pltpu.CompilerParams(vmem_limit_bytes=4 * 1024 * 1024),
    )(row, col)
    return row.reshape(users), col.reshape(per)


def solution(mesh):
    n_user, n_item = mesh.shape["user"], mesh.shape["item"]
    n_y = 1
    while n_user % (2 * n_y) == 0 and 8 * n_y * n_y <= n_user:
        n_y *= 2
    placed = (P(("item", "user"), None), P(), P(), P(("item", "user")), P("user", None), P("user"))
    return jax.shard_map(
        functools.partial(on_device, n_user, n_item, n_y),
        mesh=mesh,
        in_specs=placed,
        out_specs=(P("user"), P(("item", "user"))),
        check_vma=False,
    )
```

```python
import functools
import math

import jax
import jax.numpy as jnp
from jax import lax
from jax.experimental import pallas as pl
from jax.experimental.pallas import tpu as pltpu
from jax.sharding import PartitionSpec as P

MESH = pl.DeviceIdType.MESH
CHUNKS = 4
PARTS = 2


def kernel(n_user, n_item, n_y, x_hbm, w1_hbm, w2_hbm, lw_hbm, uv_hbm, pos_hbm, row_ref, col_ref,
           xv, w1v, w2v, uvb, uvt, posb, lwv, emb, lwg, col_part, col_send, col_recv, row_send, row_recv,
           in_sem, w1_sem, lw_ssem, lw_rsem, emb_ssem, emb_rsem, col_ssem, col_rsem,
           uv_ssem, uv_rsem, pos_ssem, pos_rsem, row_ssem, row_rsem):
    n_z = n_user // n_y
    u = lax.axis_index("user")
    i = lax.axis_index("item")
    z, y = u // n_y, u % n_y
    core = lax.rem(i, 2)
    mate = i + 1 - 2 * core
    per = xv.shape[0]
    users, d_emb = uvb.shape
    half = users // 2
    sub = d_emb // PARTS
    rows = users // 128
    inverse_temp = 4.0 / math.sqrt(d_emb)
    deep = w1v.shape[0] // CHUNKS

    cu = pltpu.make_async_copy(uv_hbm, uvb, in_sem.at[2])
    cx = pltpu.make_async_copy(x_hbm, xv, in_sem.at[0])
    cx.start()
    cw = pltpu.make_async_copy(lw_hbm, lwv, in_sem.at[4])
    cw.start()
    c1 = []
    for c in range(CHUNKS):
        part = pl.ds(c * deep, deep)
        c1.append(pltpu.make_async_copy(w1_hbm.at[part], w1v.at[part], w1_sem.at[c]))
        c1[-1].start()
        if c == 0:
            cu.start()
    c2 = pltpu.make_async_copy(w2_hbm, w2v, in_sem.at[1])
    c2.start()
    cp = pltpu.make_async_copy(pos_hbm, posb.at[0], in_sem.at[3])
    cp.start()

    def z_to(d):
        return {"user": lax.rem(z + d, n_z) * n_y + y}

    def y_to(e):
        return {"user": z * n_y + lax.rem(y + e, n_y)}

    def plane_to(k, e):
        return {"user": z * n_y + lax.rem(y + e, n_y), "item": lax.rem(i + k, n_item)}

    plane = [(k, e) for e in range(n_y - 1, -1, -1) for k in range(n_item) if (k, e) != (0, 0)]

    barrier = pltpu.get_barrier_semaphore()
    for d in range(1, n_z):
        pl.semaphore_signal(barrier, inc=1, device_id=z_to(d), device_id_type=MESH)
    for k, e in plane:
        pl.semaphore_signal(barrier, inc=1, device_id=plane_to(k, e), device_id_type=MESH)

    def remote(src, dst, ssem, rsem, to):
        return pltpu.make_async_remote_copy(src_ref=src, dst_ref=dst, send_sem=ssem, recv_sem=rsem,
                                            device_id=to, device_id_type=MESH)

    def lw_copy(d):
        return remote(lwg.at[0], lwg.at[d], lw_ssem.at[d], lw_rsem.at[d], z_to(d))

    def emb_copy(d):
        return remote(emb.at[0], emb.at[d], emb_ssem.at[d], emb_rsem.at[d], z_to(d))

    def col_copy(d):
        return remote(col_send.at[d], col_recv.at[d], col_ssem.at[d], col_rsem.at[d], z_to(n_z - d))

    def uv_copy(e, s):
        part = pl.ds(s * sub, sub)
        return remote(uvt.at[0, core, part], uvt.at[e, core, part],
                      uv_ssem.at[e, 0, s], uv_rsem.at[e, 0, s], y_to(e))

    def uv_share(e, s):
        part = pl.ds(s * sub, sub)
        return remote(uvt.at[e, core, part], uvt.at[e, core, part],
                      uv_ssem.at[e, 1, s], uv_rsem.at[e, 1, s], {"item": mate})

    def pos_copy(e):
        return remote(pos_hbm, posb.at[e], pos_ssem.at[e], pos_rsem.at[e], y_to(e))

    def row_copy(k, e):
        return remote(row_send.at[e], row_recv.at[k, e], row_ssem.at[k, e], row_rsem.at[k, e],
                      plane_to(k, e))

    lwg[0] = jnp.zeros((8, 128), jnp.float32)
    cw.wait()
    lwg[0, 0:1, 0:per] = lwv[...]

    def turn(h):
        uvt[0, h] = uvb[pl.ds(pl.multiple_of(h * half, half), half), :].T

    cx.wait()
    hidden = None
    for c in range(CHUNKS):
        c1[c].wait()
        part = jnp.dot(xv[:, c * deep:(c + 1) * deep], w1v[c * deep:(c + 1) * deep, :],
                       preferred_element_type=jnp.float32)
        hidden = part if c == 0 else hidden + part
        if c == 0:
            cu.wait()
            turn(core)
            pl.semaphore_wait(barrier, n_z - 1 + len(plane))
            for s in range(PARTS):
                for e in range(1, n_y):
                    uv_copy(e, s).start()
            for d in range(1, n_z):
                lw_copy(d).start()
            for e in range(1, n_y):
                pos_copy(e).start()
    hidden = jnp.maximum(hidden, 0.0).astype(jnp.bfloat16)
    c2.wait()
    emb[0] = jnp.dot(hidden, w2v[...], preferred_element_type=jnp.float32).astype(jnp.bfloat16)
    for d in range(1, n_z):
        emb_copy(d).start()
    turn(1 - core)

    eye = (lax.broadcasted_iota(jnp.int32, (per, 128), 0)
           == lax.broadcasted_iota(jnp.int32, (per, 128), 1))
    item_of = lax.broadcasted_iota(jnp.int32, (per, half), 0)

    def block(d, e, slot, h, carry, scores=None):
        row_max, row_sum, row_pos = carry
        if scores is None:
            scores = jnp.dot(emb[d], uvt[e, h], preferred_element_type=jnp.float32)
        scores = scores * inverse_temp
        top = jnp.max(scores, axis=1, keepdims=True)
        lse = top + jnp.log(jnp.sum(jnp.exp(scores - top), axis=1, keepdims=True))
        row = 2 * e + slot
        col_part[d, row:row + 1, :] = jnp.sum(jnp.where(eye, lse, 0.0), axis=0, keepdims=True)
        weight = jnp.sum(jnp.where(eye, lwg[d, 0:1, :], 0.0), axis=1, keepdims=True)
        logits = scores + weight
        new_max = jnp.maximum(row_max, jnp.max(logits, axis=0, keepdims=True))
        row_sum = row_sum * jnp.exp(row_max - new_max) + jnp.sum(
            jnp.exp(logits - new_max), axis=0, keepdims=True)
        start = (i * n_user + lax.rem(z + n_z - d, n_z) * n_y + y) * per
        hits = posb[e, h] == start + item_of
        row_pos = row_pos + jnp.sum(jnp.where(hits, logits, 0.0), axis=0, keepdims=True)
        return new_max, row_sum, row_pos

    def joined(parts):
        top = jnp.max(parts, axis=0, keepdims=True)
        return top + jnp.log(jnp.sum(jnp.exp(parts - top), axis=0, keepdims=True))

    def col_stats(d):
        return jnp.broadcast_to(joined(col_part[d, 0:2 * n_y, :]), (8, 128))

    def send_col(d):
        col_send[d] = col_stats(d)
        col_copy(d).start()

    def loop(low, high, step, carry):
        if n_z <= 4:
            for d in range(low, high):
                carry = step(d, carry)
            return carry
        return lax.fori_loop(low, high, step, carry)

    empty = (jnp.full((1, half), -1e30, jnp.float32), jnp.zeros((1, half), jnp.float32),
             jnp.zeros((1, half), jnp.float32))

    def own_block(d, carry):
        return tuple(block(d, 0, h, h, carry[h]) for h in range(2))

    def own_step(d, carry):
        lw_copy(d).wait_recv()
        emb_copy(d).wait_recv()
        return own_block(d, carry)

    halves = (core, 1 - core)
    cp.wait()
    own = own_block(0, (empty, empty))
    for s in range(PARTS):
        for e in range(1, n_y):
            uv_copy(e, s).wait_recv()
            uv_share(e, s).start()
    early = 2 if n_z % 2 == 0 else 1
    for d in range(1, early):
        own = own_step(d, own)
    for e in range(1, n_y):
        pos_copy(e).wait_recv()
        for s in range(PARTS):
            uv_share(e, s).wait_recv()

    rows_here = emb[0:early].reshape(early * per, d_emb)
    others = []
    for e in range(1, n_y):
        pair = []
        for k in range(2):
            scores = jnp.dot(rows_here, uvt[e, halves[k]], preferred_element_type=jnp.float32)
            carry = empty
            for d in range(early):
                carry = block(d, e, k, halves[k], carry, scores[d * per:(d + 1) * per])
            pair.append(carry)
        others.append(tuple(pair))
    for d in range(1, early):
        send_col(d)

    def full_step(j, carry):
        own, others = carry
        group = [j * early + k for k in range(early)]
        for d in group:
            lw_copy(d).wait_recv()
            emb_copy(d).wait_recv()
        rows_now = emb[pl.ds(j * early, early)].reshape(early * per, d_emb)

        def meet(e, slot, h, carry):
            scores = jnp.dot(rows_now, uvt[e, h], preferred_element_type=jnp.float32)
            for k, d in enumerate(group):
                carry = block(d, e, slot, h, carry, scores[k * per:(k + 1) * per])
            return carry

        others = tuple(tuple(meet(e, k, halves[k], others[e - 1][k]) for k in range(2))
                       for e in range(1, n_y))
        own = tuple(meet(0, h, h, own[h]) for h in range(2))
        for d in group:
            send_col(d)
        return own, others

    own, others = loop(1, n_z // early, full_step, (own, tuple(others)))
    others = list(others)
    col_recv[0] = col_stats(0)

    for e, carry in enumerate([own] + others):
        stats = [(row_max + jnp.log(row_sum), row_pos) for row_max, row_sum, row_pos in carry]
        if e > 0:
            low = [jnp.where(core == 0, a, b) for a, b in zip(*stats)]
            high = [jnp.where(core == 0, b, a) for a, b in zip(*stats)]
            stats = [low, high]
        row_send[(n_y - e) % n_y] = jnp.concatenate(
            [stats[h][m][:, 128 * k:128 * (k + 1)] for m in range(2) for h in range(2)
             for k in range(rows // 2)], axis=0)
    for k, e in plane:
        row_copy(k, e).start()
    row_recv[0, 0] = row_send[0]

    for d in range(1, n_z):
        col_copy(d).wait_recv()
    col_ref[...] = joined(col_recv[:, 0, :])[:, 0:per]

    for k, e in plane:
        row_copy(k, e).wait_recv()
    stats = row_recv[...].reshape(n_item * n_y, 2 * rows, 128)
    lse_all = stats[:, 0:rows, :]
    top = jnp.max(lse_all, axis=0)
    total = top + jnp.log(jnp.sum(jnp.exp(lse_all - top), axis=0))
    row_ref[...] = total - jnp.sum(stats[:, rows:2 * rows, :], axis=0)

    for d in range(1, n_z):
        lw_copy(d).wait_send()
        emb_copy(d).wait_send()
        col_copy(d).wait_send()
    for e in range(1, n_y):
        pos_copy(e).wait_send()
        for s in range(PARTS):
            uv_copy(e, s).wait_send()
            uv_share(e, s).wait_send()
    for k, e in plane:
        row_copy(k, e).wait_send()


def hand_out(row_in, col_in, row_out, col_out, sem):
    first = pltpu.make_async_copy(row_in, row_out, sem.at[0])
    second = pltpu.make_async_copy(col_in, col_out, sem.at[1])
    first.start()
    second.start()
    first.wait()
    second.wait()


def on_device(n_user, n_item, n_y, item_features, layer_one, layer_two, log_weight, user_vectors,
              positive_index):
    per, d_in = item_features.shape
    d_hid, d_emb = layer_two.shape
    users = user_vectors.shape[0]
    n_z = n_user // n_y
    rows = users // 128
    anywhere = pl.BlockSpec(memory_space=pltpu.HBM)
    vmem = pl.BlockSpec(memory_space=pltpu.VMEM)
    dma = pltpu.SemaphoreType.DMA
    shapes = (jax.ShapeDtypeStruct((rows, 128), jnp.float32),
              jax.ShapeDtypeStruct((1, per), jnp.float32))
    row, col = pl.pallas_call(
        functools.partial(kernel, n_user, n_item, n_y),
        out_shape=(pltpu.VMEM((rows, 128), jnp.float32), pltpu.VMEM((1, per), jnp.float32)),
        in_specs=[anywhere] * 6,
        out_specs=(vmem, vmem),
        scratch_shapes=[
            pltpu.VMEM((per, d_in), jnp.bfloat16),
            pltpu.VMEM((d_in, d_hid), jnp.bfloat16),
            pltpu.VMEM((d_hid, d_emb), jnp.bfloat16),
            pltpu.VMEM((users, d_emb), jnp.bfloat16),
            pltpu.VMEM((n_y, 2, d_emb, users // 2), jnp.bfloat16),
            pltpu.VMEM((n_y, 2, 1, users // 2), jnp.int32),
            pltpu.VMEM((1, per), jnp.float32),
            pltpu.VMEM((n_z, per, d_emb), jnp.bfloat16),
            pltpu.VMEM((n_z, 8, 128), jnp.float32),
            pltpu.VMEM((n_z, 8, 128), jnp.float32),
            pltpu.VMEM((n_z, 8, 128), jnp.float32),
            pltpu.VMEM((n_z, 8, 128), jnp.float32),
            pltpu.VMEM((n_y, 2 * rows, 128), jnp.float32),
            pltpu.VMEM((n_item, n_y, 2 * rows, 128), jnp.float32),
            dma((5,)),
            dma((CHUNKS,)),
            dma((n_z,)),
            dma((n_z,)),
            dma((n_z,)),
            dma((n_z,)),
            dma((n_z,)),
            dma((n_z,)),
            dma((n_y, 2, PARTS)),
            dma((n_y, 2, PARTS)),
            dma((n_y,)),
            dma((n_y,)),
            dma((n_item, n_y)),
            dma((n_item, n_y)),
        ],
        compiler_params=pltpu.CompilerParams(
            collective_id=0, has_side_effects=True, vmem_limit_bytes=62 * 1024 * 1024),
    )(item_features, layer_one, layer_two, log_weight.reshape(1, per), user_vectors,
      positive_index.reshape(2, 1, users // 2))
    row, col = pl.pallas_call(
        hand_out,
        out_shape=shapes,
        in_specs=[pl.BlockSpec(memory_space=pl.ANY)] * 2,
        out_specs=(anywhere, anywhere),
        scratch_shapes=[dma((2,))],
        compiler_params=pltpu.CompilerParams(vmem_limit_bytes=4 * 1024 * 1024),
    )(row, col)
    return row.reshape(users), col.reshape(per)


def solution(mesh):
    n_user, n_item = mesh.shape["user"], mesh.shape["item"]
    n_y = 1
    while n_user % (2 * n_y) == 0 and 8 * n_y * n_y <= n_user:
        n_y *= 2
    placed = (P(("item", "user"), None), P(), P(), P(("item", "user")), P("user", None), P("user"))
    return jax.shard_map(
        functools.partial(on_device, n_user, n_item, n_y),
        mesh=mesh,
        in_specs=placed,
        out_specs=(P("user"), P(("item", "user"))),
        check_vma=False,
    )
```
